256 devices in a mesh: dp: 16 (over y, x), seq: 8 (over z), tensor: 2 (over core).
Axes of the slice: x: 4, y: 4, z: 8, core: 2. Of those that a mesh axis runs over, the one named last changes fastest.
Arguments:
- queries: bfloat16 [24576, 2048], P(('dp', 'seq'), 'tensor'), may hold values from -150 to 150
- keys: bfloat16 [24576, 2048], P(('dp', 'seq'), 'tensor'), may hold values from -6 to 6
- values: bfloat16 [24576, 2048], P(('dp', 'seq'), 'tensor'), may hold values from -6 to 6
- out_grad: bfloat16 [24576, 3072], P(('dp', 'seq'), 'tensor'), may hold values from -24 to 24
- gate: float32 [16, 3072], P('dp'), may hold values from -4 to 4
- proj_weight: bfloat16 [3072, 2048], P(('dp', 'seq'), 'tensor'), may hold values from -0.125 to 0.125
- lengths: int32 [16], P('dp'), may hold values from 128 to 1536, as said below
Outputs:
- query_grad: bfloat16 [24576, 2048], P(('dp', 'seq'), 'tensor')
- key_grad: bfloat16 [24576, 2048], P(('dp', 'seq'), 'tensor')
- value_grad: bfloat16 [24576, 2048], P(('dp', 'seq'), 'tensor')
- proj_grad: float32 [3072, 2048], P(('dp', 'seq'), 'tensor')
The draws below stay inside these ranges and needn't reach their ends.
Inputs may be any that keep to these rules, and one draw needn't show every extreme that they name: `lengths`: each a multiple of 128; some sample has exactly 1536 tokens.
All inputs are finite; a program needn't handle non-finite values.
Results may differ from the reference program's by a relative error of at most 0.022.
Values may be sent and summed in bfloat16 or wider, within the bound.
No kernel may reach another device: no remote copies, remote signals or barrier semaphores. Data moves between devices by JAX's collectives and lax.ppermute only.
A program may use at most 64 MiB of HBM per device.

```python
import math
import jax
import jax.numpy as jnp
from jax import lax

D = 3072
HD = 128
HEADS = 16
GRAIN = 128
SAMPLES = 16
LMAX = 1536
TOKENS = 24576


def pair_plan(key):
    base = jnp.clip(jax.random.normal(jax.random.fold_in(key, 11), (TOKENS, HEADS * HD), jnp.float32), -6.0, 6.0)
    return base


def draw_keys(key, part):
    base = pair_plan(key)
    return base.astype(jnp.bfloat16)


def draw_queries(key, part):
    key = jax.random.fold_in(key, 1)
    own = jnp.clip(jax.random.normal(key, (TOKENS, HEADS * HD), jnp.float32), -6.0, 6.0)
    return own.astype(jnp.bfloat16)


def draw_lengths(key, part):
    key = jax.random.fold_in(key, 3)
    steps = LMAX // GRAIN
    drawn = jax.random.randint(jax.random.fold_in(key, 1), (SAMPLES,), 1, steps + 1) * GRAIN
    chosen = jax.random.randint(jax.random.fold_in(key, 2), (), 0, SAMPLES)
    return jnp.where(jnp.arange(SAMPLES, dtype=jnp.int32) == chosen, LMAX, drawn).astype(jnp.int32)


def raised(result, key, source, target, blocks, factor):
    owner, partner = [(jnp.arange(result.shape[dim]) // (result.shape[dim] // blocks)).reshape([-1 if axis == dim else 1 for axis in range(result.ndim)]) for dim in (source, target)]
    chosen = jax.random.permutation(key, blocks)[partner]
    strong = (owner == chosen) | (owner == (partner + blocks // 2) % blocks)
    return jnp.where(strong, factor * result, result)


def level_of(key, shape, cuts, smallest, largest):
    def one(axis_at, shards_of):
        draws = jax.random.uniform(jax.random.fold_in(jax.random.fold_in(key, 6), axis_at), (shards_of,), jnp.float32, smallest / len(cuts), largest / len(cuts))
        return jnp.repeat(jnp.exp(draws), shape[axis_at] // shards_of).reshape((-1,) + (1,) * (len(shape) - axis_at - 1))

    loudness = one(*cuts[0])
    for cut in cuts[1:]:
        loudness = loudness * one(*cut)
    return loudness


def noise(rng, dims, deviation, reach, cuts=(), kind=jnp.bfloat16):
    result = deviation * jax.random.normal(rng, dims, jnp.float32)
    if cuts:
        result = result * level_of(rng, dims, cuts, -0.22, 0.18)
    return jnp.clip(result, -reach, reach).astype(kind)


def gaussian_with(rng, dims, spread, reach, shards, heavy, held_as=jnp.bfloat16):
    values = spread * jax.random.normal(rng, dims, jnp.float32)
    if shards:
        values = values * level_of(rng, dims, shards, -0.22, 0.18)
    return jnp.clip(raised(values, jax.random.fold_in(rng, 3), *heavy), -reach, reach).astype(held_as)


def setup_inputs(seed: int = 0) -> dict:
    splits = jax.random.split(jax.random.key(seed), 8)
    return {
        "queries": draw_queries(jax.random.fold_in(splits[7], 71), 0),
        "keys": draw_keys(jax.random.fold_in(splits[7], 71), 0),
        "values": noise(splits[2], (TOKENS, HEADS * HD), 1.0, 6.0, ((0, 128), (1, 2))),
        "out_grad": gaussian_with(splits[3], (TOKENS, D), 1.0, 24.0, ((0, 128), (1, 2)), (0, 1, 128, 5.5)),
        "gate": noise(splits[4], (SAMPLES, D), 1.0, 4.0, ((0, 16),), jnp.float32),
        "proj_weight": noise(splits[5], (D, HEADS * HD), (HEADS * HD) ** -0.5, 0.125, ((0, 128), (1, 2))),
        "lengths": draw_lengths(jax.random.fold_in(splits[7], 71), 0),
    }


def attend_head(query, key_rows, value_rows, grad_out, key_live):
    length_all = query.shape[0]
    block = math.gcd(512, length_all)
    factor = query.shape[1] ** -0.5

    def visit(carry, number):
        key_acc, value_acc = carry
        start = number * block
        query_block = lax.dynamic_slice_in_dim(query, start, block, 0)
        grad_block = lax.dynamic_slice_in_dim(grad_out, start, block, 0)
        scores = jnp.dot(query_block, key_rows.T, preferred_element_type=jnp.float32) * factor
        scores = jnp.where(key_live[None, :], scores, -jnp.inf)
        top = jnp.max(scores, axis=1, keepdims=True)
        weights = jnp.exp(scores - top)
        probs = weights / jnp.sum(weights, axis=1, keepdims=True)
        probs_low = probs.astype(jnp.bfloat16)
        output = jnp.dot(probs_low, value_rows, preferred_element_type=jnp.float32)
        delta = jnp.sum(grad_block.astype(jnp.float32) * output, axis=1, keepdims=True)
        prob_grad = jnp.dot(grad_block, value_rows.T, preferred_element_type=jnp.float32)
        score_grad = (probs * (prob_grad - delta)).astype(jnp.bfloat16)
        query_part = jnp.dot(score_grad, key_rows, preferred_element_type=jnp.float32) * factor
        key_acc = key_acc + jnp.dot(score_grad.T, query_block, preferred_element_type=jnp.float32) * factor
        value_acc = value_acc + jnp.dot(probs_low.T, grad_block, preferred_element_type=jnp.float32)
        return (key_acc, value_acc), (output.astype(jnp.bfloat16), query_part.astype(jnp.bfloat16))

    zeros = jnp.zeros(query.shape, jnp.float32)
    (key_acc, value_acc), (outputs, query_parts) = lax.scan(visit, (zeros, zeros), jnp.arange(length_all // block, dtype=jnp.int32))
    width = query.shape[1]
    return (outputs.reshape(length_all, width), query_parts.reshape(length_all, width),
            key_acc.astype(jnp.bfloat16), value_acc.astype(jnp.bfloat16))


def reference(queries, keys, values, out_grad, gate, proj_weight, lengths):
    rows = jnp.arange(TOKENS, dtype=jnp.int32)
    sample = rows // LMAX
    live = (rows % LMAX) < lengths[sample]
    scaled_grad = jnp.where(live[:, None], out_grad.astype(jnp.float32) * gate[sample], 0.0).astype(jnp.bfloat16)
    attn_grad = jnp.dot(scaled_grad, proj_weight, preferred_element_type=jnp.float32).astype(jnp.bfloat16)

    def split(array):
        return array.reshape(SAMPLES, LMAX, HEADS, HD).transpose(0, 2, 1, 3)

    def sample_grads(packed):
        query, key_rows, value_rows, grad_out, count_live = packed
        key_live = jnp.arange(LMAX, dtype=jnp.int32) < count_live

        def head_grads(member):
            return attend_head(member[0], member[1], member[2], member[3], key_live)

        return lax.map(head_grads, (query, key_rows, value_rows, grad_out))

    results = lax.map(sample_grads, (split(queries), split(keys), split(values), split(attn_grad), lengths))

    def merge(array):
        return array.transpose(0, 2, 1, 3).reshape(TOKENS, HEADS * HD)

    attn_out, query_grad, key_grad, value_grad = [merge(array) for array in results]
    proj_grad = jnp.dot(scaled_grad.T, attn_out, preferred_element_type=jnp.float32)
    return query_grad, key_grad, value_grad, proj_grad
```

```python
import functools
import math

import jax
import jax.numpy as jnp
from jax import lax
from jax.experimental import pallas as pl
from jax.experimental.pallas import tpu as pltpu
from jax.sharding import PartitionSpec as P

HD = 128
BLOCK = 256
VMEM_LIMIT = 48 * 1024 * 1024
BF16 = jnp.bfloat16
F32 = jnp.float32
FACTOR = HD**-0.5
FACTOR_LOG2 = HD**-0.5 * math.log2(math.e)
NT = (((1,), (1,)), ((), ()))


def cost(flops, read, exps=0):
    return pl.CostEstimate(flops=int(flops), bytes_accessed=int(read), transcendentals=int(exps))


def params():
    return pltpu.CompilerParams(vmem_limit_bytes=VMEM_LIMIT)


def pack_kernel(query_ref, key_ref, value_ref, weight_ref, out_ref):
    rows = query_ref.shape[0]
    out_ref[0, 0:rows, :] = query_ref[...]
    out_ref[0, rows : 2 * rows, :] = key_ref[...]
    out_ref[0, 2 * rows : 3 * rows, :] = value_ref[...]
    weight = weight_ref[...].astype(F32)
    spare = out_ref.shape[1] - 3 * rows - weight.shape[0]
    weight = jnp.concatenate([weight, jnp.zeros((spare, HD), F32)], axis=0)
    out_ref[0, 3 * rows :, :] = weight.astype(BF16)


def pack(queries, keys, values, weight, slots):
    rows = queries.shape[0]
    wrows = weight.shape[0]
    height = 3 * rows + -(-wrows // 16) * 16
    column = pl.BlockSpec((rows, HD), lambda z: (0, z))
    return pl.pallas_call(
        pack_kernel,
        grid=(slots,),
        out_shape=jax.ShapeDtypeStruct((slots, height, HD), BF16),
        in_specs=[column, column, column, pl.BlockSpec((wrows, HD), lambda z: (0, z))],
        out_specs=pl.BlockSpec((1, height, HD), lambda z: (z, 0, 0)),
        compiler_params=params(),
        cost_estimate=cost(0, 2 * 2 * slots * height * HD),
    )(queries, keys, values, weight)


def unpack_kernel(packed_ref, query_ref, key_ref, value_ref, weight_ref):
    rows = query_ref.shape[0]
    query_ref[...] = packed_ref[0, 0:rows, :]
    key_ref[...] = packed_ref[0, rows : 2 * rows, :]
    value_ref[...] = packed_ref[0, 2 * rows : 3 * rows, :]
    weight_ref[...] = packed_ref[0, 3 * rows :, :].astype(F32)[: weight_ref.shape[0]]


def unpack(packed, rows, wrows):
    slots, height, _ = packed.shape
    column = pl.BlockSpec((rows, HD), lambda z: (0, z))
    token = jax.ShapeDtypeStruct((rows, slots * HD), BF16)
    return pl.pallas_call(
        unpack_kernel,
        grid=(slots,),
        out_shape=[token, token, token, jax.ShapeDtypeStruct((wrows, slots * HD), F32)],
        in_specs=[pl.BlockSpec((1, height, HD), lambda z: (z, 0, 0))],
        out_specs=[column, column, column, pl.BlockSpec((wrows, HD), lambda z: (0, z))],
        compiler_params=params(),
        cost_estimate=cost(0, 2 * 2 * slots * height * HD),
    )(packed)


def forward_kernel(rows, length_ref, packed_ref, probs_ref, out_ref, low_ref, value_t):
    slots = packed_ref.shape[0]
    total = slots * rows
    step = pl.program_id(0)

    @pl.when(step == 0)
    def _():
        value_t[...] = packed_ref[:, 2 * rows : 3 * rows, :].reshape(total, HD).T

    keys = packed_ref[:, rows : 2 * rows, :].reshape(total, HD)
    queries = packed_ref[:, 0:rows, :].reshape(total, HD)
    for number in range(total // BLOCK):

        @pl.when(step == number)
        def _():
            block = queries[number * BLOCK : (number + 1) * BLOCK]
            scores = lax.dot_general(keys, block, NT, preferred_element_type=F32)
            live = lax.broadcasted_iota(jnp.int32, (total, BLOCK), 0) < length_ref[0]
            scores = jnp.where(live, scores, -jnp.inf)
            top = jnp.max(scores, axis=0, keepdims=True)
            weights = jnp.exp2((scores - top) * FACTOR_LOG2)
            probs = weights * (1.0 / jnp.sum(weights, axis=0, keepdims=True))
            low = probs.astype(BF16)
            probs_ref[...] = low
            output = jnp.dot(value_t[...], low, preferred_element_type=F32)
            out_ref[...] = output
            low_ref[...] = output.astype(BF16)


def attend_forward(packed, lengths, rows):
    slots = packed.shape[0]
    total = slots * rows
    return pl.pallas_call(
        functools.partial(forward_kernel, rows),
        grid=(total // BLOCK,),
        out_shape=[
            jax.ShapeDtypeStruct((total, total), BF16),
            jax.ShapeDtypeStruct((HD, total), F32),
            jax.ShapeDtypeStruct((HD, total), BF16),
        ],
        in_specs=[
            pl.BlockSpec(memory_space=pltpu.SMEM),
            pl.BlockSpec(packed.shape, lambda i: (0, 0, 0)),
        ],
        out_specs=[
            pl.BlockSpec((total, BLOCK), lambda i: (0, i)),
            pl.BlockSpec((HD, BLOCK), lambda i: (0, i)),
            pl.BlockSpec((HD, BLOCK), lambda i: (0, i)),
        ],
        scratch_shapes=[pltpu.VMEM((HD, total), BF16)],
        compiler_params=params(),
        cost_estimate=cost(8 * total * total * HD, 2 * total * total, total * total),
    )(lengths, packed)


def project_kernel(grad_ref, weight_ref, own_ref, other_ref):
    product = jnp.dot(grad_ref[...], weight_ref[...], preferred_element_type=F32)
    own_ref[...] = product[:, :HD]
    other_ref[...] = product[:, HD:].astype(BF16)


def project(grad, weight):
    total, features = grad.shape
    return pl.pallas_call(
        project_kernel,
        grid=(total // BLOCK,),
        out_shape=[
            jax.ShapeDtypeStruct((total, HD), F32),
            jax.ShapeDtypeStruct((total, HD), BF16),
        ],
        in_specs=[
            pl.BlockSpec((BLOCK, features), lambda i: (i, 0)),
            pl.BlockSpec((features, 2 * HD), lambda i: (0, 0)),
        ],
        out_specs=[pl.BlockSpec((BLOCK, HD), lambda i: (i, 0))] * 2,
        compiler_params=params(),
        cost_estimate=cost(4 * total * features * HD, 2 * total * features),
    )(grad, weight)


def weight_grad_kernel(own_t_ref, other_t_ref, grad_ref, own_ref, other_ref):
    for source, target in ((own_t_ref, own_ref), (other_t_ref, other_ref)):
        product = jnp.dot(source[...], grad_ref[...], preferred_element_type=F32)
        target[...] = product.T.astype(BF16)


def weight_grad(own_t, other_t, grad):
    total, features = grad.shape
    return pl.pallas_call(
        weight_grad_kernel,
        grid=(features // BLOCK,),
        out_shape=[jax.ShapeDtypeStruct((features, HD), BF16)] * 2,
        in_specs=[
            pl.BlockSpec((HD, total), lambda i: (0, 0)),
            pl.BlockSpec((HD, total), lambda i: (0, 0)),
            pl.BlockSpec((total, BLOCK), lambda i: (0, i)),
        ],
        out_specs=[pl.BlockSpec((BLOCK, HD), lambda i: (i, 0))] * 2,
        compiler_params=params(),
        cost_estimate=cost(4 * total * features * HD, 2 * total * features),
    )(own_t, other_t, grad)


def backward_kernel(
    rows, packed_ref, probs_ref, out_ref, own_ref, got_ref, result_ref, key_t, query_acc, key_acc, value_acc
):
    slots = packed_ref.shape[0]
    total = slots * rows
    step = pl.program_id(0)
    keys = packed_ref[:, rows : 2 * rows, :].reshape(total, HD)

    @pl.when(step == 0)
    def _():
        key_t[...] = keys.T
        key_acc[...] = jnp.zeros_like(key_acc)
        value_acc[...] = jnp.zeros_like(value_acc)

    values = packed_ref[:, 2 * rows : 3 * rows, :].reshape(total, HD)
    queries = packed_ref[:, 0:rows, :].reshape(total, HD)
    grad = (own_ref[...] + got_ref[...].astype(F32)).astype(BF16)
    delta = jnp.sum(grad.astype(F32).T * out_ref[...], axis=0, keepdims=True)
    prob_grad = lax.dot_general(values, grad, NT, preferred_element_type=F32)
    low = probs_ref[...]
    score_grad = (low.astype(F32) * (prob_grad - delta)).astype(BF16)
    value_acc[...] += jnp.dot(low, grad, preferred_element_type=F32)
    query_t = jnp.dot(key_t[...], score_grad, preferred_element_type=F32) * FACTOR
    for number in range(total // BLOCK):

        @pl.when(step == number)
        def _():
            block = queries[number * BLOCK : (number + 1) * BLOCK]
            key_acc[...] += jnp.dot(score_grad, block, preferred_element_type=F32)
            query_acc[number * BLOCK : (number + 1) * BLOCK, :] = query_t.T.astype(BF16)

    @pl.when(step == total // BLOCK - 1)
    def _():
        result_ref[:, 0:rows, :] = query_acc[...].reshape(slots, rows, HD)
        result_ref[:, rows : 2 * rows, :] = (
            (key_acc[...] * FACTOR).astype(BF16).reshape(slots, rows, HD)
        )
        result_ref[:, 2 * rows : 3 * rows, :] = value_acc[...].astype(BF16).reshape(slots, rows, HD)


def attend_backward(packed, probs, out, own, got, rows):
    slots = packed.shape[0]
    total = slots * rows
    return pl.pallas_call(
        functools.partial(backward_kernel, rows),
        grid=(total // BLOCK,),
        out_shape=jax.ShapeDtypeStruct((slots, 3 * rows, HD), BF16),
        in_specs=[
            pl.BlockSpec(packed.shape, lambda i: (0, 0, 0)),
            pl.BlockSpec((total, BLOCK), lambda i: (0, i)),
            pl.BlockSpec((HD, BLOCK), lambda i: (0, i)),
            pl.BlockSpec((BLOCK, HD), lambda i: (i, 0)),
            pl.BlockSpec((BLOCK, HD), lambda i: (i, 0)),
        ],
        out_specs=pl.BlockSpec((slots, 3 * rows, HD), lambda i: (0, 0, 0)),
        scratch_shapes=[
            pltpu.VMEM((HD, total), BF16),
            pltpu.VMEM((total, HD), BF16),
            pltpu.VMEM((total, HD), F32),
            pltpu.VMEM((total, HD), F32),
        ],
        compiler_params=params(),
        cost_estimate=cost(8 * total * total * HD, 2 * total * total),
    )(packed, probs, out, own, got)


def per_device(queries, keys, values, out_grad, gate, proj_weight, lengths):
    seq = lax.axis_size("seq")
    rows = queries.shape[0]
    half = out_grad.shape[1]
    wrows = proj_weight.shape[0]
    core = lax.axis_index("tensor")
    swap = [(0, 1), (1, 0)]

    position = lax.axis_index("seq") * rows + jnp.arange(rows, dtype=jnp.int32)
    live = position < lengths[0]
    gate_here = lax.dynamic_slice_in_dim(gate, core * half, half, 1)
    scaled = jnp.where(live[:, None], out_grad.astype(F32) * gate_here, 0.0).astype(BF16)
    grad = lax.all_gather(scaled, "seq", axis=0, tiled=True)

    packed = lax.all_to_all(
        pack(queries, keys, values, proj_weight, seq), "seq", split_axis=0, concat_axis=0, tiled=True
    )
    weight_rows = packed[:, 3 * rows : 3 * rows + wrows].reshape(seq * wrows, HD)
    weight_head = lax.all_gather(weight_rows, "dp", axis=0, tiled=True)
    weight_own = lax.dynamic_slice_in_dim(weight_head, core * half, half, 0)
    weight_send = lax.dynamic_slice_in_dim(weight_head, (1 - core) * half, half, 0)
    weight_other = lax.ppermute(weight_send, "tensor", swap)
    weight = jnp.concatenate([weight_own, weight_other], axis=1)

    probs, out, low = attend_forward(packed, lengths, rows)
    low_other = lax.ppermute(low, "tensor", swap)

    own, other = project(grad, weight)
    got = lax.ppermute(other, "tensor", swap)

    proj_own, proj_send = weight_grad(low, low_other, grad)
    proj_got = lax.ppermute(proj_send, "tensor", swap)
    first = jnp.where(core == 0, proj_own, proj_got)
    second = jnp.where(core == 0, proj_got, proj_own)
    parts = jnp.concatenate([first, second], axis=0).reshape(-1, seq * wrows, HD)
    parts = lax.all_to_all(parts, "dp", split_axis=0, concat_axis=0, tiled=True)

    grads = attend_backward(packed, probs, out, own, got, rows)
    proj = jnp.sum(parts.astype(F32), axis=0).astype(BF16).reshape(seq, wrows, HD)
    spare = packed.shape[1] - 3 * rows - wrows
    result = jnp.concatenate([grads, proj, jnp.zeros((seq, spare, HD), BF16)], axis=1)
    result = lax.all_to_all(result, "seq", split_axis=0, concat_axis=0, tiled=True)
    return tuple(unpack(result, rows, wrows))


def solution(mesh):
    token = P(("dp", "seq"), "tensor")
    return jax.shard_map(
        per_device,
        mesh=mesh,
        in_specs=(token, token, token, token, P("dp", None), token, P("dp")),
        out_specs=(token, token, token, token),
        check_vma=False,
    )
```

```python
import functools
import math

import jax
import jax.numpy as jnp
from jax import lax
from jax.experimental import pallas as pl
from jax.experimental.pallas import tpu as pltpu
from jax.sharding import PartitionSpec as P

HD = 128
PAIR = 2
FBLOCK = 256
VMEM_LIMIT = 48 * 1024 * 1024
BF16 = jnp.bfloat16
F32 = jnp.float32
FACTOR = HD**-0.5
FACTOR_LOG2 = HD**-0.5 * math.log2(math.e)
NT = (((1,), (1,)), ((), ()))
OFFSETS = (-1, 1, -2, 2, -3, 3, 0, 4)
GROUPS = ((0, 4), (4, 6), (6, 8))


def cost(flops, read, exps=0):
    return pl.CostEstimate(flops=int(flops), bytes_accessed=int(read), transcendentals=int(exps))


def params():
    return pltpu.CompilerParams(vmem_limit_bytes=VMEM_LIMIT)


def whole(array):
    zeros = (0,) * array.ndim
    return pl.BlockSpec(array.shape, lambda *_: zeros)


def smem():
    return pl.BlockSpec(memory_space=pltpu.SMEM)


def scale_kernel(length_ref, grad_ref, gate_ref, out_ref):
    rows, half = grad_ref.shape
    start = pl.multiple_of(lax.axis_index("tensor") * half, HD)
    gate = gate_ref[:, pl.ds(start, half)]
    left = length_ref[0] - lax.axis_index("seq") * rows
    live = lax.broadcasted_iota(jnp.int32, (rows, 1), 0) < left
    out_ref[...] = jnp.where(live, grad_ref[...].astype(F32) * gate, 0.0).astype(BF16)


def scale(out_grad, gate, lengths):
    return pl.pallas_call(
        scale_kernel,
        out_shape=jax.ShapeDtypeStruct(out_grad.shape, BF16),
        in_specs=[smem(), whole(out_grad), whole(gate)],
        out_specs=whole(out_grad),
        compiler_params=params(),
        cost_estimate=cost(0, 4 * out_grad.size),
    )(lengths, out_grad, gate)


def pack_kernel(query_ref, key_ref, value_ref, weight_ref, out_ref):
    rows = query_ref.shape[0]
    out_ref[0, 0:rows, :] = query_ref[...]
    out_ref[0, rows : 2 * rows, :] = key_ref[...]
    out_ref[0, 2 * rows : 3 * rows, :] = value_ref[...]
    weight = weight_ref[...].astype(F32)
    spare = out_ref.shape[1] - 3 * rows - weight.shape[0]
    weight = jnp.concatenate([weight, jnp.zeros((spare, HD), F32)], axis=0)
    out_ref[0, 3 * rows :, :] = weight.astype(BF16)


def pack(queries, keys, values, weight, slots):
    rows = queries.shape[0]
    wrows = weight.shape[0]
    height = 3 * rows + -(-wrows // 16) * 16
    column = pl.BlockSpec((rows, HD), lambda z: (0, z))
    return pl.pallas_call(
        pack_kernel,
        grid=(slots,),
        out_shape=jax.ShapeDtypeStruct((slots, height, HD), BF16),
        in_specs=[column, column, column, pl.BlockSpec((wrows, HD), lambda z: (0, z))],
        out_specs=pl.BlockSpec((1, height, HD), lambda z: (z, 0, 0)),
        compiler_params=params(),
        cost_estimate=cost(0, 2 * 2 * slots * height * HD),
    )(queries, keys, values, weight)


def unpack_kernel(packed_ref, query_ref, key_ref, value_ref, weight_ref):
    rows = query_ref.shape[0]
    query_ref[...] = packed_ref[0, 0:rows, :]
    key_ref[...] = packed_ref[0, rows : 2 * rows, :]
    value_ref[...] = packed_ref[0, 2 * rows : 3 * rows, :]
    weight_ref[...] = packed_ref[0, 3 * rows :, :].astype(F32)[: weight_ref.shape[0]]


def unpack(packed, rows, wrows):
    slots, height, _ = packed.shape
    column = pl.BlockSpec((rows, HD), lambda z: (0, z))
    token = jax.ShapeDtypeStruct((rows, slots * HD), BF16)
    return pl.pallas_call(
        unpack_kernel,
        grid=(slots,),
        out_shape=[token, token, token, jax.ShapeDtypeStruct((wrows, slots * HD), F32)],
        in_specs=[pl.BlockSpec((1, height, HD), lambda z: (z, 0, 0))],
        out_specs=[column, column, column, pl.BlockSpec((wrows, HD), lambda z: (0, z))],
        compiler_params=params(),
        cost_estimate=cost(0, 2 * 2 * slots * height * HD),
    )(packed)


def slot_of(number, slots):
    even = number % 2 == 0
    distance = number // 2 + 1
    offset = jnp.where(even, slots - distance, distance)
    offset = jnp.where(number == 6, 0, jnp.where(number == 7, 4, offset))
    return lax.rem(lax.axis_index("seq") + offset, slots)


def forward_kernel(rows, length_ref, packed_ref, weights_ref, inverse_ref, out_ref, low_ref, value_t):
    slots = packed_ref.shape[0]
    total = slots * rows
    step = pl.program_id(0)

    @pl.when(step == 0)
    def _():
        value_t[...] = packed_ref[:, 2 * rows : 3 * rows, :].reshape(total, HD).T

    keys = packed_ref[:, rows : 2 * rows, :].reshape(total, HD)
    block = jnp.concatenate(
        [packed_ref[slot_of(PAIR * step + i, slots), 0:rows, :] for i in range(PAIR)], axis=0
    )
    scores = lax.dot_general(keys, block, NT, preferred_element_type=F32)
    live = lax.broadcasted_iota(jnp.int32, (total, 1), 0) < length_ref[0]
    scores = jnp.where(live, scores, -jnp.inf)
    top = jnp.max(scores, axis=0, keepdims=True)
    weights = jnp.exp2((scores - top) * FACTOR_LOG2)
    inverse = 1.0 / jnp.sum(weights, axis=0, keepdims=True)
    inverse_ref[...] = inverse
    weights = weights.astype(BF16)
    weights_ref[...] = weights
    output = jnp.dot(value_t[...], weights, preferred_element_type=F32) * inverse
    out_ref[...] = output
    low_ref[...] = output.astype(BF16)


def attend_forward(packed, lengths, rows):
    slots = packed.shape[0]
    total = slots * rows
    width = PAIR * rows
    return pl.pallas_call(
        functools.partial(forward_kernel, rows),
        grid=(slots // PAIR,),
        out_shape=[
            jax.ShapeDtypeStruct((total, total), BF16),
            jax.ShapeDtypeStruct((1, total), F32),
            jax.ShapeDtypeStruct((HD, total), F32),
            jax.ShapeDtypeStruct((HD, total), BF16),
        ],
        in_specs=[smem(), whole(packed)],
        out_specs=[
            pl.BlockSpec((total, width), lambda i: (0, i)),
            pl.BlockSpec((1, width), lambda i: (0, i)),
            pl.BlockSpec((HD, width), lambda i: (0, i)),
            pl.BlockSpec((HD, width), lambda i: (0, i)),
        ],
        scratch_shapes=[pltpu.VMEM((HD, total), BF16)],
        compiler_params=params(),
        cost_estimate=cost(4 * total * total * HD, 2 * total * total, total * total),
    )(lengths, packed)


def project_kernel(*refs):
    *grads, weight_ref, own_ref, other_ref = refs
    start = 0
    for grad in grads:
        product = jnp.dot(grad[...], weight_ref[...], preferred_element_type=F32)
        stop = start + grad.shape[0]
        own_ref[start:stop, :] = product[:, :HD]
        other_ref[start:stop, :] = product[:, HD:].astype(BF16)
        start = stop


def project(grads, weight):
    total = sum(grad.shape[0] for grad in grads)
    features = weight.shape[0]
    shapes = [jax.ShapeDtypeStruct((total, HD), F32), jax.ShapeDtypeStruct((total, HD), BF16)]
    return pl.pallas_call(
        project_kernel,
        out_shape=shapes,
        in_specs=[whole(array) for array in (*grads, weight)],
        out_specs=[whole(shape) for shape in shapes],
        compiler_params=params(),
        cost_estimate=cost(4 * total * features * HD, 2 * total * features),
    )(*grads, weight)


def weight_grad_kernel(own_t_ref, other_t_ref, *refs):
    *grads, own_ref, other_ref = refs
    outputs = jnp.concatenate([own_t_ref[...], other_t_ref[...]], axis=0)
    grad = jnp.concatenate([grad[...] for grad in grads], axis=0)
    product = jnp.dot(outputs, grad, preferred_element_type=F32)
    own_ref[...] = product[:HD].T.astype(BF16)
    other_ref[...] = product[HD:].T.astype(BF16)


def weight_grad(own_t, other_t, grads):
    total = own_t.shape[1]
    features = grads[0].shape[1]
    return pl.pallas_call(
        weight_grad_kernel,
        grid=(features // FBLOCK,),
        out_shape=[jax.ShapeDtypeStruct((features, HD), BF16)] * 2,
        in_specs=[whole(own_t), whole(other_t)]
        + [pl.BlockSpec((grad.shape[0], FBLOCK), lambda i: (0, i)) for grad in grads],
        out_specs=[pl.BlockSpec((FBLOCK, HD), lambda i: (i, 0))] * 2,
        compiler_params=params(),
        cost_estimate=cost(4 * total * features * HD, 2 * total * features),
    )(own_t, other_t, *grads)


def backward_kernel(rows, group, first, last, *refs):
    packed_ref, weights_ref, inverse_ref, out_ref, own_ref, got_ref, *refs = refs
    slots = packed_ref.shape[0]
    total = slots * rows
    width = PAIR * rows
    start, stop = group
    steps = (stop - start) // PAIR
    step = pl.program_id(0)
    sums, refs = ((), refs) if first else (refs[:2], refs[2:])
    if last:
        *before, result_ref, key_t, query_acc, key_acc, value_acc = refs
    else:
        query_acc, key_acc, value_acc, key_t = refs
    keys = packed_ref[:, rows : 2 * rows, :].reshape(total, HD)

    @pl.when(step == 0)
    def _():
        key_t[...] = keys.T
        key_acc[...] = jnp.zeros_like(key_acc) if first else sums[0][...]
        value_acc[...] = jnp.zeros_like(value_acc) if first else sums[1][...]

    values = packed_ref[:, 2 * rows : 3 * rows, :].reshape(total, HD)
    block = jnp.concatenate(
        [packed_ref[slot_of(start + PAIR * step + i, slots), 0:rows, :] for i in range(PAIR)], axis=0
    )
    grad = (own_ref[...] + got_ref[...].astype(F32)).astype(BF16)
    delta = jnp.sum(grad.astype(F32).T * out_ref[...], axis=0, keepdims=True)
    inverse = inverse_ref[...]
    prob_grad = lax.dot_general(values, grad, NT, preferred_element_type=F32)
    weights = weights_ref[...]
    score_grad = (weights.astype(F32) * ((prob_grad - delta) * inverse)).astype(BF16)
    scaled = (grad.astype(F32).T * inverse).T.astype(BF16)
    value_acc[...] += jnp.dot(weights, scaled, preferred_element_type=F32)
    key_acc[...] += jnp.dot(score_grad, block, preferred_element_type=F32)
    query_t = jnp.dot(key_t[...], score_grad, preferred_element_type=F32) * FACTOR
    query_acc[pl.ds(pl.multiple_of(step * width, width), width), :] = query_t.T.astype(BF16)

    if last:

        @pl.when(step == steps - 1)
        def _():
            number = 0
            for source in (*before, query_acc):
                for place in range(0, source.shape[0], rows):
                    result_ref[slot_of(number, slots), 0:rows, :] = source[place : place + rows, :]
                    number += 1
            result_ref[:, rows : 2 * rows, :] = (
                (key_acc[...] * FACTOR).astype(BF16).reshape(slots, rows, HD)
            )
            result_ref[:, 2 * rows : 3 * rows, :] = (
                value_acc[...].astype(BF16).reshape(slots, rows, HD)
            )


def attend_backward(packed, state, own, got, rows, group, done, sums):
    weights, inverse, out = state
    slots = packed.shape[0]
    total = slots * rows
    width = PAIR * rows
    start, stop = group
    size = (stop - start) * rows
    first, last = not sums, stop == slots
    shift = start // PAIR
    sum_shapes = [jax.ShapeDtypeStruct((total, HD), F32)] * 2
    if last:
        shapes = [jax.ShapeDtypeStruct((slots, 3 * rows, HD), BF16)]
        scratch = [pltpu.VMEM((size, HD), BF16)] + [pltpu.VMEM((total, HD), F32)] * 2
    else:
        shapes = [jax.ShapeDtypeStruct((size, HD), BF16), *sum_shapes]
        scratch = []
    extra = [*sums, *done] if last else list(sums)
    return pl.pallas_call(
        functools.partial(backward_kernel, rows, group, first, last),
        grid=((stop - start) // PAIR,),
        out_shape=shapes,
        in_specs=[
            whole(packed),
            pl.BlockSpec((total, width), lambda i: (0, i + shift)),
            pl.BlockSpec((1, width), lambda i: (0, i + shift)),
            pl.BlockSpec((HD, width), lambda i: (0, i + shift)),
            pl.BlockSpec((width, HD), lambda i: (i, 0)),
            pl.BlockSpec((width, HD), lambda i: (i, 0)),
            *[whole(array) for array in extra],
        ],
        out_specs=[whole(shape) for shape in shapes],
        scratch_shapes=[pltpu.VMEM((HD, total), BF16), *scratch],
        compiler_params=params(),
        cost_estimate=cost(8 * total * size * HD, 2 * total * size),
    )(packed, weights, inverse, out, own, got, *extra)


def per_device(queries, keys, values, out_grad, gate, proj_weight, lengths):
    seq = lax.axis_size("seq")
    rows = queries.shape[0]
    half = out_grad.shape[1]
    wrows = proj_weight.shape[0]
    core = lax.axis_index("tensor")
    swap = [(0, 1), (1, 0)]
    right = [(i, (i + 1) % seq) for i in range(seq)]
    left = [(i, (i - 1) % seq) for i in range(seq)]

    own_rows = scale(out_grad, gate, lengths)
    from_left, from_right = [own_rows], [own_rows]
    for _ in range(3):
        from_left.append(lax.ppermute(from_left[-1], "seq", right))
        from_right.append(lax.ppermute(from_right[-1], "seq", left))
    far = [
        lax.ppermute(from_left[3][: rows // 2], "seq", right),
        lax.ppermute(from_right[3][rows // 2 :], "seq", left),
    ]
    blocks = [[array] for i in range(1, 4) for array in (from_left[i], from_right[i])] + [[own_rows], far]

    packed = lax.all_to_all(
        pack(queries, keys, values, proj_weight, seq), "seq", split_axis=0, concat_axis=0, tiled=True
    )
    weight_rows = packed[:, 3 * rows : 3 * rows + wrows].reshape(1, seq * wrows, HD)
    copies = jnp.broadcast_to(weight_rows, (lax.axis_size("dp"), seq * wrows, HD))
    weight_head = lax.all_to_all(copies, "dp", split_axis=0, concat_axis=0, tiled=True).reshape(-1, HD)
    weight_own = lax.dynamic_slice_in_dim(weight_head, core * half, half, 0)
    weight_send = lax.dynamic_slice_in_dim(weight_head, (1 - core) * half, half, 0)
    weight_other = lax.ppermute(weight_send, "tensor", swap)
    weight = jnp.concatenate([weight_own, weight_other], axis=1)

    *state, low = attend_forward(packed, lengths, rows)
    low_other = lax.ppermute(low, "tensor", swap)

    done, sums = [], []
    for start, stop in GROUPS:
        own, other = project(sum(blocks[start:stop], []), weight)
        got = lax.ppermute(other, "tensor", swap)
        query_rows, *sums = attend_backward(packed, state, own, got, rows, (start, stop), done, sums)
        done.append(query_rows)
    grads = done[-1]

    proj_own, proj_send = weight_grad(low, low_other, sum(blocks, []))
    proj_got = lax.ppermute(proj_send, "tensor", swap)
    first = jnp.where(core == 0, proj_own, proj_got)
    second = jnp.where(core == 0, proj_got, proj_own)
    parts = jnp.concatenate([first, second], axis=0).reshape(-1, seq * wrows, HD)
    parts = lax.all_to_all(parts, "dp", split_axis=0, concat_axis=0, tiled=True)

    proj = jnp.sum(parts.astype(F32), axis=0).astype(BF16).reshape(seq, wrows, HD)
    spare = packed.shape[1] - 3 * rows - wrows
    result = jnp.concatenate([grads, proj, jnp.zeros((seq, spare, HD), BF16)], axis=1)
    result = lax.all_to_all(result, "seq", split_axis=0, concat_axis=0, tiled=True)
    return tuple(unpack(result, rows, wrows))


def solution(mesh):
    token = P(("dp", "seq"), "tensor")
    return jax.shard_map(
        per_device,
        mesh=mesh,
        in_specs=(token, token, token, token, P("dp", None), token, P("dp")),
        out_specs=(token, token, token, token),
        check_vma=False,
    )
```

```python
import functools
import math

import jax
import jax.numpy as jnp
from jax import lax
from jax.experimental import pallas as pl
from jax.experimental.pallas import tpu as pltpu
from jax.sharding import PartitionSpec as P

HD = 128
PAIR = 2
FBLOCK = 256
MIB = 1024 * 1024
BF16 = jnp.bfloat16
F32 = jnp.float32
FACTOR = HD**-0.5
FACTOR_LOG2 = HD**-0.5 * math.log2(math.e)
NT = (((1,), (1,)), ((), ()))


def cost(flops, read, exps=0):
    return pl.CostEstimate(flops=int(flops), bytes_accessed=int(read), transcendentals=int(exps))


def params(limit=48):
    return pltpu.CompilerParams(vmem_limit_bytes=limit * MIB)


def whole(array):
    zeros = (0,) * array.ndim
    return pl.BlockSpec(array.shape, lambda *_: zeros)


def smem():
    return pl.BlockSpec(memory_space=pltpu.SMEM)


def scale_kernel(length_ref, grad_ref, gate_ref, out_ref):
    rows, half = grad_ref.shape
    start = pl.multiple_of(lax.axis_index("tensor") * half, HD)
    gate = gate_ref[:, pl.ds(start, half)]
    left = length_ref[0] - lax.axis_index("seq") * rows
    live = lax.broadcasted_iota(jnp.int32, (rows, 1), 0) < left
    out_ref[...] = jnp.where(live, grad_ref[...].astype(F32) * gate, 0.0).astype(BF16)


def scale(out_grad, gate, lengths):
    return pl.pallas_call(
        scale_kernel,
        out_shape=jax.ShapeDtypeStruct(out_grad.shape, BF16),
        in_specs=[smem(), whole(out_grad), whole(gate)],
        out_specs=whole(out_grad),
        compiler_params=params(),
        cost_estimate=cost(0, 4 * out_grad.size),
    )(lengths, out_grad, gate)


def anywhere():
    return pl.BlockSpec(memory_space=pl.ANY)


def corner(array):
    zeros = (0,) * array.ndim
    return pl.BlockSpec((1,) * (array.ndim - 2) + (16, HD), lambda *_: zeros)


def pack_kernel(query_ref, key_ref, value_ref, weight_ref, out_ref, sems):
    rows = query_ref.shape[0]
    slots, height, _ = out_ref.shape
    copies = []
    for slot in range(slots):
        for i, ref in enumerate((query_ref, key_ref, value_ref)):
            source = ref.at[:, slot * HD : (slot + 1) * HD]
            target = out_ref.at[slot, i * rows : (i + 1) * rows, :]
            copies.append(pltpu.make_async_copy(source, target, sems.at[len(copies)]))
    for copy in copies:
        copy.start()
    weight = weight_ref[...].astype(F32)
    spare = height - 3 * rows - weight.shape[0]
    weight = jnp.concatenate([weight, jnp.zeros((spare, weight.shape[1]), F32)], axis=0).astype(BF16)
    for slot in range(slots):
        out_ref[slot, 3 * rows : height, :] = weight[:, slot * HD : (slot + 1) * HD]
    for copy in copies:
        copy.wait()


def pack(queries, keys, values, weight, slots):
    rows = queries.shape[0]
    wrows = weight.shape[0]
    shape = jax.ShapeDtypeStruct((slots, 3 * rows + -(-wrows // 16) * 16, HD), BF16)
    return pl.pallas_call(
        pack_kernel,
        out_shape=shape,
        in_specs=[anywhere(), anywhere(), anywhere(), whole(weight)],
        out_specs=whole(shape),
        scratch_shapes=[pltpu.SemaphoreType.DMA((3 * slots,))],
        compiler_params=params(60),
        cost_estimate=cost(0, 4 * shape.size),
    )(queries, keys, values, weight)


def unpack_kernel(packed_ref, query_ref, key_ref, value_ref, weight_ref, padded, sems):
    rows = query_ref.shape[0]
    slots, height, _ = packed_ref.shape
    wrows = weight_ref.shape[0]
    first = pltpu.make_async_copy(packed_ref.at[:, 3 * rows : height, :], padded, sems.at[0])
    first.start()
    copies = []
    for slot in range(slots):
        for i, ref in enumerate((query_ref, key_ref, value_ref)):
            source = packed_ref.at[slot, i * rows : (i + 1) * rows, :]
            target = ref.at[:, slot * HD : (slot + 1) * HD]
            copies.append(pltpu.make_async_copy(source, target, sems.at[len(copies) + 1]))
    for copy in copies:
        copy.start()
    first.wait()
    for slot in range(slots):
        weight_ref[:, slot * HD : (slot + 1) * HD] = padded[slot].astype(F32)[:wrows]
    for copy in copies:
        copy.wait()


def unpack(packed, rows, wrows):
    slots, height, _ = packed.shape
    token = jax.ShapeDtypeStruct((rows, slots * HD), BF16)
    weight = jax.ShapeDtypeStruct((wrows, slots * HD), F32)
    return pl.pallas_call(
        unpack_kernel,
        out_shape=[token, token, token, weight],
        in_specs=[anywhere()],
        out_specs=[anywhere(), anywhere(), anywhere(), whole(weight)],
        scratch_shapes=[
            pltpu.VMEM((slots, height - 3 * rows, HD), BF16),
            pltpu.SemaphoreType.DMA((3 * slots + 1,)),
        ],
        compiler_params=params(),
        cost_estimate=cost(0, 2 * 2 * slots * height * HD),
    )(packed)


def finish_kernel(grads_ref, parts_ref, out_ref, padded, sem):
    _, wrows, _ = parts_ref.shape
    slots, height, _ = out_ref.shape
    spare = padded.shape[1]
    total = parts_ref[0].astype(F32)
    for i in range(1, parts_ref.shape[0]):
        total += parts_ref[i].astype(F32)
    total = total.reshape(slots, wrows // slots, HD)
    zeros = jnp.zeros((spare - wrows // slots, HD), F32)
    for slot in range(slots):
        padded[slot] = jnp.concatenate([total[slot], zeros], axis=0).astype(BF16)
    copy = pltpu.make_async_copy(padded, out_ref.at[:, height - spare : height, :], sem)
    copy.start()
    copy.wait()


def finish(grads, parts, spare):
    return pl.pallas_call(
        finish_kernel,
        out_shape=jax.ShapeDtypeStruct(grads.shape, grads.dtype),
        in_specs=[anywhere(), whole(parts)],
        out_specs=anywhere(),
        scratch_shapes=[pltpu.VMEM((grads.shape[0], spare, HD), BF16), pltpu.SemaphoreType.DMA(())],
        input_output_aliases={0: 0},
        compiler_params=params(),
        cost_estimate=cost(0, 2 * parts.size),
    )(grads, parts)


def slot_of(number, slots):
    even = number % 2 == 0
    distance = number // 2 + 1
    offset = jnp.where(even, slots - distance, distance)
    offset = jnp.where(number == 6, 0, jnp.where(number == 7, 4, offset))
    return lax.rem(lax.axis_index("seq") + offset, slots)


def forward_kernel(rows, length_ref, packed_ref, _, weights_ref, inverse_ref, out_ref, low_ref, value_t):
    slots = packed_ref.shape[0]
    total = slots * rows
    step = pl.program_id(0)

    @pl.when(step == 0)
    def _():
        value_t[...] = packed_ref[:, 2 * rows : 3 * rows, :].reshape(total, HD).T

    keys = packed_ref[:, rows : 2 * rows, :].reshape(total, HD)
    block = jnp.concatenate(
        [packed_ref[slot_of(PAIR * step + i, slots), 0:rows, :] for i in range(PAIR)], axis=0
    )
    scores = lax.dot_general(keys, block, NT, preferred_element_type=F32)
    live = lax.broadcasted_iota(jnp.int32, (total, 1), 0) < length_ref[0]
    scores = jnp.where(live, scores, -jnp.inf)
    top = jnp.max(scores, axis=0, keepdims=True)
    weights = jnp.exp2((scores - top) * FACTOR_LOG2)
    inverse = 1.0 / jnp.sum(weights, axis=0, keepdims=True)
    inverse_ref[...] = inverse
    weights = weights.astype(BF16)
    weights_ref[...] = weights
    output = jnp.dot(value_t[...], weights, preferred_element_type=F32) * inverse
    out_ref[...] = output
    low_ref[...] = output.astype(BF16)


def attend_forward(packed, lengths, rows, after):
    slots = packed.shape[0]
    total = slots * rows
    width = PAIR * rows
    return pl.pallas_call(
        functools.partial(forward_kernel, rows),
        grid=(slots // PAIR,),
        out_shape=[
            jax.ShapeDtypeStruct((total, total), BF16),
            jax.ShapeDtypeStruct((1, total), F32),
            jax.ShapeDtypeStruct((HD, total), F32),
            jax.ShapeDtypeStruct((HD, total), BF16),
        ],
        in_specs=[smem(), whole(packed), corner(after)],
        out_specs=[
            pl.BlockSpec((total, width), lambda i: (0, i)),
            pl.BlockSpec((1, width), lambda i: (0, i)),
            pl.BlockSpec((HD, width), lambda i: (0, i)),
            pl.BlockSpec((HD, width), lambda i: (0, i)),
        ],
        scratch_shapes=[pltpu.VMEM((HD, total), BF16)],
        compiler_params=params(),
        cost_estimate=cost(4 * total * total * HD, 2 * total * total, total * total),
    )(lengths, packed, after)


def project_kernel(*refs):
    *grads, own_weight_ref, other_weight_ref, _, own_ref, other_ref = refs
    half = grads[0].shape[1]
    core = lax.axis_index("tensor")
    mine = pl.ds(pl.multiple_of(core * half, half), half)
    weight = jnp.concatenate([own_weight_ref[mine, :], other_weight_ref[mine, :]], axis=1)
    start = 0
    for grad in grads:
        product = jnp.dot(grad[...], weight, preferred_element_type=F32)
        stop = start + grad.shape[0]
        own_ref[start:stop, :] = product[:, :HD]
        other_ref[start:stop, :] = product[:, HD:].astype(BF16)
        start = stop


def project(grads, own_weight, other_weight, after):
    total = sum(grad.shape[0] for grad in grads)
    features = grads[0].shape[1]
    shapes = [jax.ShapeDtypeStruct((total, HD), F32), jax.ShapeDtypeStruct((total, HD), BF16)]
    return pl.pallas_call(
        project_kernel,
        grid=(1,),
        out_shape=shapes,
        in_specs=[whole(array) for array in (*grads, own_weight, other_weight)] + [corner(after)],
        out_specs=[whole(shape) for shape in shapes],
        compiler_params=params(),
        cost_estimate=cost(4 * total * features * HD, 2 * total * features),
    )(*grads, own_weight, other_weight, after)


def weight_grad_kernel(group, final, *refs):
    start, stop = group
    own_t_ref, other_t_ref, *refs = refs
    if final:
        *grads, sum_ref, own_ref, other_ref = refs
    else:
        *grads, sum_ref = refs
    outputs = jnp.concatenate([own_t_ref[:, start:stop], other_t_ref[:, start:stop]], axis=0)
    features = grads[0].shape[1]
    for begin in range(0, features, FBLOCK):
        columns = slice(begin, begin + FBLOCK)
        grad = jnp.concatenate([grad[:, columns] for grad in grads], axis=0)
        product = jnp.dot(outputs, grad, preferred_element_type=F32)
        if final:
            product = (product + sum_ref[:, columns]).T.astype(BF16)
            own_ref[columns, :] = product[:, :HD]
            other_ref[columns, :] = product[:, HD:]
        else:
            sum_ref[:, columns] = product


def weight_grad(own_t, other_t, grads, group, before):
    features = grads[0].shape[1]
    final = before is not None
    if final:
        shapes = [jax.ShapeDtypeStruct((features, HD), BF16)] * 2
    else:
        shapes = [jax.ShapeDtypeStruct((2 * HD, features), F32)]
    inputs = [own_t, other_t, *grads] + ([before] if final else [])
    return pl.pallas_call(
        functools.partial(weight_grad_kernel, group, final),
        out_shape=shapes,
        in_specs=[whole(array) for array in inputs],
        out_specs=[whole(shape) for shape in shapes],
        compiler_params=params(),
        cost_estimate=cost(4 * (group[1] - group[0]) * features * HD, 2 * (group[1] - group[0]) * features),
    )(*inputs)


def hold_kernel(*_):
    pass


def hold(arrays, micros):
    return pl.pallas_call(
        hold_kernel,
        out_shape=[jax.ShapeDtypeStruct(array.shape, array.dtype) for array in arrays],
        in_specs=[anywhere()] * len(arrays),
        out_specs=[anywhere()] * len(arrays),
        input_output_aliases={i: i for i in range(len(arrays))},
        cost_estimate=pl.CostEstimate(flops=int(micros * 1e9), bytes_accessed=int(micros * 3e6), transcendentals=0),
    )(*arrays)


def halves_kernel(left_ref, right_ref, first_ref, second_ref):
    half = first_ref.shape[0]
    first_ref[...] = left_ref[:half]
    second_ref[...] = right_ref[half:]


def halves(left, right):
    half, features = left.shape[0] // 2, left.shape[1]
    shape = jax.ShapeDtypeStruct((half, features), BF16)
    return pl.pallas_call(
        halves_kernel,
        out_shape=[shape, shape],
        in_specs=[whole(left), whole(right)],
        out_specs=[whole(shape), whole(shape)],
        compiler_params=params(),
        cost_estimate=cost(0, 4 * left.size),
    )(left, right)


def join_kernel(own_ref, got_ref, _, out_ref):
    core = lax.axis_index("tensor")
    count = out_ref.shape[0] // 2
    out_ref[pl.ds(core * count, count)] = own_ref[...].reshape(count, *out_ref.shape[1:])
    out_ref[pl.ds((1 - core) * count, count)] = got_ref[...].reshape(count, *out_ref.shape[1:])


def join(own, got, slots, after):
    shape = jax.ShapeDtypeStruct((slots, 2 * own.shape[0] // slots, HD), BF16)
    return pl.pallas_call(
        join_kernel,
        grid=(1,),
        out_shape=shape,
        in_specs=[whole(own), whole(got), corner(after)],
        out_specs=whole(shape),
        compiler_params=params(),
        cost_estimate=cost(0, 8 * own.size),
    )(own, got, after)


def backward_kernel(rows, start, first, last, *refs):
    packed_ref, weights_ref, inverse_ref, out_ref, own_ref, got_ref, _, *refs = refs
    slots = packed_ref.shape[0]
    total = slots * rows
    width = PAIR * rows
    step = pl.program_id(0)
    if last:
        *sums, done_ref, result_ref, key_t, query_acc, key_acc, value_acc = refs
    else:
        query_acc, key_acc, value_acc, key_t = refs
    keys = packed_ref[:, rows : 2 * rows, :].reshape(total, HD)

    @pl.when(step == 0)
    def _():
        key_t[...] = keys.T
        key_acc[...] = jnp.zeros_like(key_acc) if first else sums[0][...]
        value_acc[...] = jnp.zeros_like(value_acc) if first else sums[1][...]

    here = pl.ds(pl.multiple_of(step * width, width), width)
    values = packed_ref[:, 2 * rows : 3 * rows, :].reshape(total, HD)
    block = jnp.concatenate(
        [packed_ref[slot_of(start + PAIR * step + i, slots), 0:rows, :] for i in range(PAIR)], axis=0
    )
    grad = (own_ref[...] + got_ref[...].astype(F32)).astype(BF16)
    grad_t = grad.astype(F32).T
    inverse = inverse_ref[...]
    delta = jnp.sum(grad_t * out_ref[...], axis=0, keepdims=True)
    prob_grad = lax.dot_general(values, grad, NT, preferred_element_type=F32)
    weights = weights_ref[...]
    score_grad = (weights.astype(F32) * ((prob_grad - delta) * inverse)).astype(BF16)
    scaled = (grad_t * inverse).T.astype(BF16)
    value_acc[...] += jnp.dot(weights, scaled, preferred_element_type=F32)
    key_acc[...] += jnp.dot(score_grad, block, preferred_element_type=F32)
    query_t = jnp.dot(key_t[...], score_grad, preferred_element_type=F32) * FACTOR
    query_acc[here, :] = query_t.T.astype(BF16)

    if last:

        @pl.when(step == pl.num_programs(0) - 1)
        def _():
            number = 0
            for source in (done_ref, query_acc):
                for place in range(0, source.shape[0], rows):
                    result_ref[slot_of(number, slots), 0:rows, :] = source[place : place + rows, :]
                    number += 1
            result_ref[:, rows : 2 * rows, :] = (
                (key_acc[...] * FACTOR).astype(BF16).reshape(slots, rows, HD)
            )
            result_ref[:, 2 * rows : 3 * rows, :] = (
                value_acc[...].astype(BF16).reshape(slots, rows, HD)
            )


def attend_backward(packed, state, own, got, rows, start, before, after):
    weights, inverse, out = state
    slots = packed.shape[0]
    total = slots * rows
    width = PAIR * rows
    size = own.shape[0]
    first, last = start == 0, start * rows + size == total
    shift = start // PAIR
    sums = [jax.ShapeDtypeStruct((total, HD), F32)] * 2
    if last:
        shapes = [jax.ShapeDtypeStruct(packed.shape, BF16)]
        scratch = [pltpu.VMEM((size, HD), BF16)] + [pltpu.VMEM((total, HD), F32)] * 2
    else:
        shapes = [jax.ShapeDtypeStruct((size, HD), BF16), *sums]
        scratch = []
    return pl.pallas_call(
        functools.partial(backward_kernel, rows, start, first, last),
        grid=(size // width,),
        out_shape=shapes,
        in_specs=[
            whole(packed),
            pl.BlockSpec((total, width), lambda i: (0, i + shift)),
            pl.BlockSpec((1, width), lambda i: (0, i + shift)),
            pl.BlockSpec((HD, width), lambda i: (0, i + shift)),
            pl.BlockSpec((width, HD), lambda i: (i, 0)),
            pl.BlockSpec((width, HD), lambda i: (i, 0)),
            corner(after),
            *[whole(array) for array in before],
        ],
        out_specs=[whole(shape) for shape in shapes],
        scratch_shapes=[pltpu.VMEM((HD, total), BF16), *scratch],
        compiler_params=params(),
        cost_estimate=cost(8 * total * size * HD, 2 * total * size),
    )(packed, weights, inverse, out, own, got, after, *before)


def per_device(queries, keys, values, out_grad, gate, proj_weight, lengths):
    seq, dp = lax.axis_size("seq"), lax.axis_size("dp")
    rows = queries.shape[0]
    wrows = proj_weight.shape[0]
    swap = [(0, 1), (1, 0)]
    right = [(i, (i + 1) % seq) for i in range(seq)]
    left = [(i, (i - 1) % seq) for i in range(seq)]

    own_rows = scale(out_grad, gate, lengths)
    from_left, from_right = [own_rows], [own_rows]
    for i in range(2):
        from_left.append(lax.ppermute(from_left[-1], "seq", right))
        from_right.append(lax.ppermute(from_right[-1], "seq", left))
        if i == 0:
            from_left[1], from_right[1] = hold((from_left[1], from_right[1]), 40)

    packed = lax.all_to_all(
        pack(queries, keys, values, proj_weight, seq), "seq", split_axis=0, concat_axis=0, tiled=True
    )
    weight_rows = packed[:, 3 * rows : 3 * rows + wrows].reshape(1, seq * wrows, HD)
    copies = jnp.broadcast_to(weight_rows, (dp, seq * wrows, HD))
    own_weight = lax.all_to_all(copies, "dp", split_axis=0, concat_axis=0, tiled=True).reshape(-1, HD)
    other_weight = lax.ppermute(own_weight, "tensor", swap)

    *state, low = attend_forward(packed, lengths, rows, copies)
    low_other = lax.ppermute(low, "tensor", swap)

    from_left.append(lax.ppermute(from_left[-1], "seq", right))
    from_right.append(lax.ppermute(from_right[-1], "seq", left))
    far_left, far_right, low = lax.optimization_barrier((from_left[3], from_right[3], low))
    far_left, far_right = halves(far_left, far_right)
    far = [lax.ppermute(far_left, "seq", right), lax.ppermute(far_right, "seq", left)]
    near = [array for i in range(1, 4) for array in (from_left[i], from_right[i])]
    last = [own_rows, *far]
    cut, total = 6 * rows, seq * rows

    own, other = project(near, own_weight, other_weight, far_left)
    got = lax.ppermute(other, "tensor", swap)
    proj_sum = weight_grad(low, low_other, near, (0, cut), None)[0]
    query_rows, *sums = attend_backward(packed, state, own, got, rows, 0, [], proj_sum)

    proj_own, proj_send = weight_grad(low, low_other, last, (cut, total), proj_sum)
    proj_got = lax.ppermute(proj_send, "tensor", swap)
    own, other = project(last, own_weight, other_weight, proj_own)
    got = lax.ppermute(other, "tensor", swap)
    joined = join(proj_own, proj_got, dp, own)
    parts = lax.all_to_all(joined, "dp", split_axis=0, concat_axis=0, tiled=True)

    grads = attend_backward(packed, state, own, got, rows, 6, [*sums, query_rows], joined)[0]
    result = finish(grads, parts, packed.shape[1] - 3 * rows)
    result = lax.all_to_all(result, "seq", split_axis=0, concat_axis=0, tiled=True)
    return tuple(unpack(result, rows, wrows))


def solution(mesh):
    token = P(("dp", "seq"), "tensor")
    return jax.shard_map(
        per_device,
        mesh=mesh,
        in_specs=(token, token, token, token, P("dp", None), token, P("dp")),
        out_specs=(token, token, token, token),
        check_vma=False,
    )
```

```python
import functools
import math

import jax
import jax.numpy as jnp
from jax import lax
from jax.experimental import pallas as pl
from jax.experimental.pallas import tpu as pltpu
from jax.sharding import PartitionSpec as P

HD = 128
HOLD1, HOLD2, HOLD3, PACK = 100, 100, 100, 24
PAIR = 2
FBLOCK = 256
MIB = 1024 * 1024
BF16 = jnp.bfloat16
F32 = jnp.float32
FACTOR = HD**-0.5
FACTOR_LOG2 = HD**-0.5 * math.log2(math.e)
NT = (((1,), (1,)), ((), ()))


def cost(flops, read, exps=0):
    return pl.CostEstimate(flops=int(flops), bytes_accessed=int(read), transcendentals=int(exps))


def long_cost(micros):
    return cost(micros * 1e9, micros * 3e6)


def params(limit=48):
    return pltpu.CompilerParams(vmem_limit_bytes=limit * MIB)


def whole(array):
    zeros = (0,) * array.ndim
    return pl.BlockSpec(array.shape, lambda *_: zeros)


def smem():
    return pl.BlockSpec(memory_space=pltpu.SMEM)


def scale_kernel(length_ref, grad_ref, gate_ref, out_ref):
    rows, half = grad_ref.shape
    start = pl.multiple_of(lax.axis_index("tensor") * half, HD)
    gate = gate_ref[:, pl.ds(start, half)]
    left = length_ref[0] - lax.axis_index("seq") * rows
    live = lax.broadcasted_iota(jnp.int32, (rows, 1), 0) < left
    out_ref[...] = jnp.where(live, grad_ref[...].astype(F32) * gate, 0.0).astype(BF16)


def scale(out_grad, gate, lengths):
    return pl.pallas_call(
        scale_kernel,
        out_shape=jax.ShapeDtypeStruct(out_grad.shape, BF16),
        in_specs=[smem(), whole(out_grad), whole(gate)],
        out_specs=whole(out_grad),
        compiler_params=params(),
        cost_estimate=cost(0, 4 * out_grad.size),
    )(lengths, out_grad, gate)


def anywhere():
    return pl.BlockSpec(memory_space=pl.ANY)


def corner(array):
    zeros = (0,) * array.ndim
    return pl.BlockSpec((1,) * (array.ndim - 2) + (16, HD), lambda *_: zeros)


def pack_kernel(query_ref, key_ref, value_ref, weight_ref, out_ref):
    rows = query_ref.shape[0]
    slots, height, _ = out_ref.shape
    weight = weight_ref[...].astype(F32)
    spare = height - 3 * rows - weight.shape[0]
    weight = jnp.concatenate([weight, jnp.zeros((spare, weight.shape[1]), F32)], axis=0).astype(BF16)
    for slot in range(slots):
        columns = slice(slot * HD, (slot + 1) * HD)
        for i, ref in enumerate((query_ref, key_ref, value_ref)):
            out_ref[slot, i * rows : (i + 1) * rows, :] = ref[:, columns]
        out_ref[slot, 3 * rows : height, :] = weight[:, columns]


def pack(queries, keys, values, weight, slots):
    rows = queries.shape[0]
    wrows = weight.shape[0]
    shape = jax.ShapeDtypeStruct((slots, 3 * rows + -(-wrows // 16) * 16, HD), BF16)
    return pl.pallas_call(
        pack_kernel,
        out_shape=shape,
        in_specs=[whole(queries), whole(keys), whole(values), whole(weight)],
        out_specs=whole(shape),
        compiler_params=params(PACK),
        cost_estimate=cost(0, 4 * shape.size),
    )(queries, keys, values, weight)


def unpack_kernel(packed_ref, query_ref, key_ref, value_ref, weight_ref, padded, sems):
    rows = query_ref.shape[0]
    slots, height, _ = packed_ref.shape
    wrows = weight_ref.shape[0]
    first = pltpu.make_async_copy(packed_ref.at[:, 3 * rows : height, :], padded, sems.at[0])
    first.start()
    copies = []
    for slot in range(slots):
        for i, ref in enumerate((query_ref, key_ref, value_ref)):
            source = packed_ref.at[slot, i * rows : (i + 1) * rows, :]
            target = ref.at[:, slot * HD : (slot + 1) * HD]
            copies.append(pltpu.make_async_copy(source, target, sems.at[len(copies) + 1]))
    for copy in copies:
        copy.start()
    first.wait()
    for slot in range(slots):
        weight_ref[:, slot * HD : (slot + 1) * HD] = padded[slot].astype(F32)[:wrows]
    for copy in copies:
        copy.wait()


def unpack(packed, rows, wrows):
    slots, height, _ = packed.shape
    token = jax.ShapeDtypeStruct((rows, slots * HD), BF16)
    weight = jax.ShapeDtypeStruct((wrows, slots * HD), F32)
    return pl.pallas_call(
        unpack_kernel,
        out_shape=[token, token, token, weight],
        in_specs=[anywhere()],
        out_specs=[anywhere(), anywhere(), anywhere(), whole(weight)],
        scratch_shapes=[
            pltpu.VMEM((slots, height - 3 * rows, HD), BF16),
            pltpu.SemaphoreType.DMA((3 * slots + 1,)),
        ],
        compiler_params=params(),
        cost_estimate=cost(0, 2 * 2 * slots * height * HD),
    )(packed)


def finish_kernel(grads_ref, parts_ref, out_ref, padded, sem):
    _, wrows, _ = parts_ref.shape
    slots, height, _ = out_ref.shape
    spare = padded.shape[1]
    total = parts_ref[0].astype(F32)
    for i in range(1, parts_ref.shape[0]):
        total += parts_ref[i].astype(F32)
    total = total.reshape(slots, wrows // slots, HD)
    zeros = jnp.zeros((spare - wrows // slots, HD), F32)
    for slot in range(slots):
        padded[slot] = jnp.concatenate([total[slot], zeros], axis=0).astype(BF16)
    copy = pltpu.make_async_copy(padded, out_ref.at[:, height - spare : height, :], sem)
    copy.start()
    copy.wait()


def finish(grads, parts, spare):
    return pl.pallas_call(
        finish_kernel,
        out_shape=jax.ShapeDtypeStruct(grads.shape, grads.dtype),
        in_specs=[anywhere(), whole(parts)],
        out_specs=anywhere(),
        scratch_shapes=[pltpu.VMEM((grads.shape[0], spare, HD), BF16), pltpu.SemaphoreType.DMA(())],
        input_output_aliases={0: 0},
        compiler_params=params(),
        cost_estimate=cost(0, 2 * parts.size),
    )(grads, parts)


def slot_of(number, slots):
    even = number % 2 == 0
    distance = number // 2 + 1
    offset = jnp.where(even, slots - distance, distance)
    offset = jnp.where(number == 6, 0, jnp.where(number == 7, 4, offset))
    return lax.rem(lax.axis_index("seq") + offset, slots)


def forward_kernel(rows, length_ref, packed_ref, _, weights_ref, inverse_ref, out_ref, low_ref, value_t):
    slots = packed_ref.shape[0]
    total = slots * rows
    step = pl.program_id(0)

    @pl.when(step == 0)
    def _():
        value_t[...] = packed_ref[:, 2 * rows : 3 * rows, :].reshape(total, HD).T

    keys = packed_ref[:, rows : 2 * rows, :].reshape(total, HD)
    block = jnp.concatenate(
        [packed_ref[slot_of(PAIR * step + i, slots), 0:rows, :] for i in range(PAIR)], axis=0
    )
    scores = lax.dot_general(keys, block, NT, preferred_element_type=F32)
    live = lax.broadcasted_iota(jnp.int32, (total, 1), 0) < length_ref[0]
    scores = jnp.where(live, scores, -jnp.inf)
    top = jnp.max(scores, axis=0, keepdims=True)
    weights = jnp.exp2((scores - top) * FACTOR_LOG2)
    inverse = 1.0 / jnp.sum(weights, axis=0, keepdims=True)
    inverse_ref[...] = inverse
    weights = weights.astype(BF16)
    weights_ref[...] = weights
    output = jnp.dot(value_t[...], weights, preferred_element_type=F32) * inverse
    out_ref[...] = output
    low_ref[...] = output.astype(BF16)


def attend_forward(packed, lengths, rows, after):
    slots = packed.shape[0]
    total = slots * rows
    width = PAIR * rows
    return pl.pallas_call(
        functools.partial(forward_kernel, rows),
        grid=(slots // PAIR,),
        out_shape=[
            jax.ShapeDtypeStruct((total, total), BF16),
            jax.ShapeDtypeStruct((1, total), F32),
            jax.ShapeDtypeStruct((HD, total), F32),
            jax.ShapeDtypeStruct((HD, total), BF16),
        ],
        in_specs=[smem(), whole(packed), corner(after)],
        out_specs=[
            pl.BlockSpec((total, width), lambda i: (0, i)),
            pl.BlockSpec((1, width), lambda i: (0, i)),
            pl.BlockSpec((HD, width), lambda i: (0, i)),
            pl.BlockSpec((HD, width), lambda i: (0, i)),
        ],
        scratch_shapes=[pltpu.VMEM((HD, total), BF16)],
        compiler_params=params(),
        cost_estimate=cost(4 * total * total * HD, 2 * total * total, total * total),
    )(lengths, packed, after)


def project_kernel(*refs):
    *grads, own_weight_ref, other_weight_ref, _, own_ref, other_ref = refs
    half = grads[0].shape[1]
    core = lax.axis_index("tensor")
    mine = pl.ds(pl.multiple_of(core * half, half), half)
    weight = jnp.concatenate([own_weight_ref[mine, :], other_weight_ref[mine, :]], axis=1)
    start = 0
    for grad in grads:
        product = jnp.dot(grad[...], weight, preferred_element_type=F32)
        stop = start + grad.shape[0]
        own_ref[start:stop, :] = product[:, :HD]
        other_ref[start:stop, :] = product[:, HD:].astype(BF16)
        start = stop


def project(grads, own_weight, other_weight, after):
    total = sum(grad.shape[0] for grad in grads)
    features = grads[0].shape[1]
    shapes = [jax.ShapeDtypeStruct((total, HD), F32), jax.ShapeDtypeStruct((total, HD), BF16)]
    return pl.pallas_call(
        project_kernel,
        grid=(1,),
        out_shape=shapes,
        in_specs=[whole(array) for array in (*grads, own_weight, other_weight)] + [corner(after)],
        out_specs=[whole(shape) for shape in shapes],
        compiler_params=params(),
        cost_estimate=cost(4 * total * features * HD, 2 * total * features),
    )(*grads, own_weight, other_weight, after)


def weight_grad_kernel(group, final, *refs):
    start, stop = group
    own_t_ref, other_t_ref, _, *refs = refs
    if final:
        *grads, sum_ref, own_ref, other_ref = refs
    else:
        *grads, sum_ref = refs
    outputs = jnp.concatenate([own_t_ref[:, start:stop], other_t_ref[:, start:stop]], axis=0)
    features = grads[0].shape[1]
    for begin in range(0, features, FBLOCK):
        columns = slice(begin, begin + FBLOCK)
        grad = jnp.concatenate([grad[:, columns] for grad in grads], axis=0)
        product = jnp.dot(outputs, grad, preferred_element_type=F32)
        if final:
            product = (product + sum_ref[:, columns]).T.astype(BF16)
            own_ref[columns, :] = product[:, :HD]
            other_ref[columns, :] = product[:, HD:]
        else:
            sum_ref[:, columns] = product


def weight_grad(own_t, other_t, grads, group, before, after):
    features = grads[0].shape[1]
    final = before is not None
    if final:
        shapes = [jax.ShapeDtypeStruct((features, HD), BF16)] * 2
    else:
        shapes = [jax.ShapeDtypeStruct((2 * HD, features), F32)]
    inputs = [*grads] + ([before] if final else [])
    return pl.pallas_call(
        functools.partial(weight_grad_kernel, group, final),
        grid=(1,),
        out_shape=shapes,
        in_specs=[whole(own_t), whole(other_t), corner(after)] + [whole(array) for array in inputs],
        out_specs=[whole(shape) for shape in shapes],
        compiler_params=params(),
        cost_estimate=cost(4 * (group[1] - group[0]) * features * HD, 2 * (group[1] - group[0]) * features),
    )(own_t, other_t, after, *inputs)


def hold_kernel(*refs):
    count = len(refs) // 2
    for source, target in zip(refs[:count], refs[count:]):
        target[...] = source[...]


def hold(arrays, micros):
    return pl.pallas_call(
        hold_kernel,
        out_shape=[jax.ShapeDtypeStruct(array.shape, array.dtype) for array in arrays],
        in_specs=[whole(array) for array in arrays],
        out_specs=[whole(array) for array in arrays],
        compiler_params=params(24),
        cost_estimate=long_cost(micros),
    )(*arrays)


def halves_kernel(left_ref, right_ref, *part_refs):
    half = left_ref.shape[0] // 2
    for ref, parts in ((left_ref, part_refs[:2]), (right_ref, part_refs[2:])):
        parts[0][...] = ref[:half]
        parts[1][...] = ref[half:]


def halves(left, right):
    half, features = left.shape[0] // 2, left.shape[1]
    shape = jax.ShapeDtypeStruct((half, features), BF16)
    return pl.pallas_call(
        halves_kernel,
        out_shape=[shape] * 4,
        in_specs=[whole(left), whole(right)],
        out_specs=[whole(shape)] * 4,
        compiler_params=params(),
        cost_estimate=long_cost(HOLD1),
    )(left, right)


def join_kernel(own_ref, got_ref, _, out_ref, sems):
    core = lax.axis_index("tensor")
    rows = own_ref.shape[0]
    first = pltpu.make_async_copy(own_ref, out_ref.at[pl.ds(core * rows, rows)], sems.at[0])
    second = pltpu.make_async_copy(got_ref, out_ref.at[pl.ds((1 - core) * rows, rows)], sems.at[1])
    first.start()
    second.start()
    first.wait()
    second.wait()


def join(own, got, after):
    return pl.pallas_call(
        join_kernel,
        grid=(1,),
        out_shape=jax.ShapeDtypeStruct((2 * own.shape[0], HD), BF16),
        in_specs=[whole(own), whole(got), corner(after)],
        out_specs=anywhere(),
        scratch_shapes=[pltpu.SemaphoreType.DMA((2,))],
        compiler_params=params(),
        cost_estimate=cost(0, 8 * own.size),
    )(own, got, after)


def backward_kernel(rows, start, first, last, *refs):
    packed_ref, weights_ref, inverse_ref, out_ref, own_ref, got_ref, _, *refs = refs
    slots = packed_ref.shape[0]
    total = slots * rows
    width = PAIR * rows
    step = pl.program_id(0)
    if last:
        *sums, done_ref, result_ref, key_t, query_acc, key_acc, value_acc = refs
    else:
        query_acc, key_acc, value_acc, key_t = refs
    keys = packed_ref[:, rows : 2 * rows, :].reshape(total, HD)

    @pl.when(step == 0)
    def _():
        key_t[...] = keys.T
        key_acc[...] = jnp.zeros_like(key_acc) if first else sums[0][...]
        value_acc[...] = jnp.zeros_like(value_acc) if first else sums[1][...]

    here = pl.ds(pl.multiple_of(step * width, width), width)
    values = packed_ref[:, 2 * rows : 3 * rows, :].reshape(total, HD)
    block = jnp.concatenate(
        [packed_ref[slot_of(start + PAIR * step + i, slots), 0:rows, :] for i in range(PAIR)], axis=0
    )
    grad = (own_ref[...] + got_ref[...].astype(F32)).astype(BF16)
    grad_t = grad.astype(F32).T
    inverse = inverse_ref[...]
    delta = jnp.sum(grad_t * out_ref[...], axis=0, keepdims=True)
    prob_grad = lax.dot_general(values, grad, NT, preferred_element_type=F32)
    weights = weights_ref[...]
    score_grad = (weights.astype(F32) * ((prob_grad - delta) * inverse)).astype(BF16)
    scaled = (grad_t * inverse).T.astype(BF16)
    value_acc[...] += jnp.dot(weights, scaled, preferred_element_type=F32)
    key_acc[...] += jnp.dot(score_grad, block, preferred_element_type=F32)
    query_t = jnp.dot(key_t[...], score_grad, preferred_element_type=F32) * FACTOR
    query_acc[here, :] = query_t.T.astype(BF16)

    if last:

        @pl.when(step == pl.num_programs(0) - 1)
        def _():
            number = 0
            for source in (done_ref, query_acc):
                for place in range(0, source.shape[0], rows):
                    result_ref[slot_of(number, slots), 0:rows, :] = source[place : place + rows, :]
                    number += 1
            result_ref[:, rows : 2 * rows, :] = (
                (key_acc[...] * FACTOR).astype(BF16).reshape(slots, rows, HD)
            )
            result_ref[:, 2 * rows : 3 * rows, :] = (
                value_acc[...].astype(BF16).reshape(slots, rows, HD)
            )


def attend_backward(packed, state, own, got, rows, start, before, after):
    weights, inverse, out = state
    slots = packed.shape[0]
    total = slots * rows
    width = PAIR * rows
    size = own.shape[0]
    first, last = start == 0, start * rows + size == total
    shift = start // PAIR
    sums = [jax.ShapeDtypeStruct((total, HD), F32)] * 2
    if last:
        shapes = [jax.ShapeDtypeStruct(packed.shape, BF16)]
        scratch = [pltpu.VMEM((size, HD), BF16)] + [pltpu.VMEM((total, HD), F32)] * 2
    else:
        shapes = [jax.ShapeDtypeStruct((size, HD), BF16), *sums]
        scratch = []
    return pl.pallas_call(
        functools.partial(backward_kernel, rows, start, first, last),
        grid=(size // width,),
        out_shape=shapes,
        in_specs=[
            whole(packed),
            pl.BlockSpec((total, width), lambda i: (0, i + shift)),
            pl.BlockSpec((1, width), lambda i: (0, i + shift)),
            pl.BlockSpec((HD, width), lambda i: (0, i + shift)),
            pl.BlockSpec((width, HD), lambda i: (i, 0)),
            pl.BlockSpec((width, HD), lambda i: (i, 0)),
            corner(after),
            *[whole(array) for array in before],
        ],
        out_specs=[whole(shape) for shape in shapes],
        scratch_shapes=[pltpu.VMEM((HD, total), BF16), *scratch],
        compiler_params=params(),
        cost_estimate=cost(8 * total * size * HD, 2 * total * size),
    )(packed, weights, inverse, out, own, got, after, *before)


def per_device(queries, keys, values, out_grad, gate, proj_weight, lengths):
    seq, dp = lax.axis_size("seq"), lax.axis_size("dp")
    rows = queries.shape[0]
    wrows = proj_weight.shape[0]
    swap = [(0, 1), (1, 0)]
    right = [(i, (i + 1) % seq) for i in range(seq)]
    left = [(i, (i - 1) % seq) for i in range(seq)]

    def move(array, step):
        return lax.ppermute(array, "seq", right if step > 0 else left)

    own_rows = scale(out_grad, gate, lengths)
    from_left, from_right = move(own_rows, 1), move(own_rows, -1)
    near = [from_left, from_right]
    left_top, left_low, right_top, right_low = halves(from_left, from_right)
    for i in range(2):
        left_top, right_low = move(left_top, 1), move(right_low, -1)
        left_low, right_top = move(left_low, 1), move(right_top, -1)
        if (HOLD2, HOLD3)[i]:
            left_top, right_low = hold((left_top, right_low), (HOLD2, HOLD3)[i])
        near += [left_top, left_low, right_top, right_low]

    packed = lax.all_to_all(
        pack(queries, keys, values, proj_weight, seq), "seq", split_axis=0, concat_axis=0, tiled=True
    )
    weight_rows = packed[:, 3 * rows : 3 * rows + wrows].reshape(1, seq * wrows, HD)
    copies = jnp.broadcast_to(weight_rows, (dp, seq * wrows, HD))
    own_weight = lax.all_to_all(copies, "dp", split_axis=0, concat_axis=0, tiled=True).reshape(-1, HD)
    other_weight = lax.ppermute(own_weight, "tensor", swap)

    *state, low = attend_forward(packed, lengths, rows, copies)
    low_other = lax.ppermute(low, "tensor", swap)

    left_top, right_low, low = lax.optimization_barrier((left_top, right_low, low))
    far = [move(left_top, 1), move(right_low, -1)]
    last = [own_rows, *far]
    cut, total = 6 * rows, seq * rows

    proj_sum = weight_grad(low, low_other, near, (0, cut), None, left_top)[0]
    near_own, other = project(near, own_weight, other_weight, proj_sum)
    near_got = lax.ppermute(other, "tensor", swap)

    proj_own, proj_send = weight_grad(low, low_other, last, (cut, total), proj_sum, near_own)
    proj_got = lax.ppermute(proj_send, "tensor", swap)
    own, other = project(last, own_weight, other_weight, proj_own)
    got = lax.ppermute(other, "tensor", swap)
    joined = join(proj_own, proj_got, own).reshape(dp, seq * wrows, HD)
    parts = lax.all_to_all(joined, "dp", split_axis=0, concat_axis=0, tiled=True)

    query_rows, *sums = attend_backward(packed, state, near_own, near_got, rows, 0, [], joined)
    grads = attend_backward(packed, state, own, got, rows, 6, [*sums, query_rows], joined)[0]
    result = finish(grads, parts, packed.shape[1] - 3 * rows)
    result = lax.all_to_all(result, "seq", split_axis=0, concat_axis=0, tiled=True)
    return tuple(unpack(result, rows, wrows))


def solution(mesh):
    token = P(("dp", "seq"), "tensor")
    return jax.shard_map(
        per_device,
        mesh=mesh,
        in_specs=(token, token, token, token, P("dp", None), token, P("dp")),
        out_specs=(token, token, token, token),
        check_vma=False,
    )
```

```python
import functools
import math

import jax
import jax.numpy as jnp
from jax import lax
from jax.experimental import pallas as pl
from jax.experimental.pallas import tpu as pltpu
from jax.sharding import PartitionSpec as P

HD = 128
HOLD1, HOLD2, HOLD3, PACK = 100, 100, 100, 24
PAIR = 2
FBLOCK = 256
MIB = 1024 * 1024
BF16 = jnp.bfloat16
F32 = jnp.float32
FACTOR = HD**-0.5
FACTOR_LOG2 = HD**-0.5 * math.log2(math.e)
NT = (((1,), (1,)), ((), ()))


def cost(flops, read, exps=0):
    return pl.CostEstimate(flops=int(flops), bytes_accessed=int(read), transcendentals=int(exps))


def long_cost(micros):
    return cost(micros * 1e9, micros * 3e6)


def params(limit=48):
    return pltpu.CompilerParams(vmem_limit_bytes=limit * MIB)


def whole(array):
    zeros = (0,) * array.ndim
    return pl.BlockSpec(array.shape, lambda *_: zeros)


def smem():
    return pl.BlockSpec(memory_space=pltpu.SMEM)


def scale_kernel(length_ref, grad_ref, gate_ref, out_ref):
    rows, half = grad_ref.shape
    start = pl.multiple_of(lax.axis_index("tensor") * half, HD)
    gate = gate_ref[:, pl.ds(start, half)]
    left = length_ref[0] - lax.axis_index("seq") * rows
    live = lax.broadcasted_iota(jnp.int32, (rows, 1), 0) < left
    out_ref[...] = jnp.where(live, grad_ref[...].astype(F32) * gate, 0.0).astype(BF16)


def scale(out_grad, gate, lengths):
    return pl.pallas_call(
        scale_kernel,
        out_shape=jax.ShapeDtypeStruct(out_grad.shape, BF16),
        in_specs=[smem(), whole(out_grad), whole(gate)],
        out_specs=whole(out_grad),
        compiler_params=params(),
        cost_estimate=cost(0, 4 * out_grad.size),
    )(lengths, out_grad, gate)


def anywhere():
    return pl.BlockSpec(memory_space=pl.ANY)


def corner(array):
    zeros = (0,) * array.ndim
    return pl.BlockSpec((1,) * (array.ndim - 2) + (16, HD), lambda *_: zeros)


def pack_kernel(query_ref, key_ref, value_ref, weight_ref, out_ref):
    rows = query_ref.shape[0]
    slots, height, _ = out_ref.shape
    weight = weight_ref[...].astype(F32)
    spare = height - 3 * rows - weight.shape[0]
    weight = jnp.concatenate([weight, jnp.zeros((spare, weight.shape[1]), F32)], axis=0).astype(BF16)
    for slot in range(slots):
        columns = slice(slot * HD, (slot + 1) * HD)
        for i, ref in enumerate((query_ref, key_ref, value_ref)):
            out_ref[slot, i * rows : (i + 1) * rows, :] = ref[:, columns]
        out_ref[slot, 3 * rows : height, :] = weight[:, columns]


def pack(queries, keys, values, weight, slots):
    rows = queries.shape[0]
    wrows = weight.shape[0]
    shape = jax.ShapeDtypeStruct((slots, 3 * rows + -(-wrows // 16) * 16, HD), BF16)
    return pl.pallas_call(
        pack_kernel,
        out_shape=shape,
        in_specs=[whole(queries), whole(keys), whole(values), whole(weight)],
        out_specs=whole(shape),
        compiler_params=params(PACK),
        cost_estimate=cost(0, 4 * shape.size),
    )(queries, keys, values, weight)


def unpack_kernel(packed_ref, query_ref, key_ref, value_ref, weight_ref, padded, sems):
    rows = query_ref.shape[0]
    slots, height, _ = packed_ref.shape
    wrows = weight_ref.shape[0]
    first = pltpu.make_async_copy(packed_ref.at[:, 3 * rows : height, :], padded, sems.at[0])
    first.start()
    copies = []
    for slot in range(slots):
        for i, ref in enumerate((query_ref, key_ref, value_ref)):
            source = packed_ref.at[slot, i * rows : (i + 1) * rows, :]
            target = ref.at[:, slot * HD : (slot + 1) * HD]
            copies.append(pltpu.make_async_copy(source, target, sems.at[len(copies) + 1]))
    for copy in copies:
        copy.start()
    first.wait()
    for slot in range(slots):
        weight_ref[:, slot * HD : (slot + 1) * HD] = padded[slot].astype(F32)[:wrows]
    for copy in copies:
        copy.wait()


def unpack(packed, rows, wrows):
    slots, height, _ = packed.shape
    token = jax.ShapeDtypeStruct((rows, slots * HD), BF16)
    weight = jax.ShapeDtypeStruct((wrows, slots * HD), F32)
    return pl.pallas_call(
        unpack_kernel,
        out_shape=[token, token, token, weight],
        in_specs=[anywhere()],
        out_specs=[anywhere(), anywhere(), anywhere(), whole(weight)],
        scratch_shapes=[
            pltpu.VMEM((slots, height - 3 * rows, HD), BF16),
            pltpu.SemaphoreType.DMA((3 * slots + 1,)),
        ],
        compiler_params=params(),
        cost_estimate=cost(0, 2 * 2 * slots * height * HD),
    )(packed)


def finish_kernel(grads_ref, parts_ref, out_ref, padded, sem):
    _, wrows, _ = parts_ref.shape
    slots, height, _ = out_ref.shape
    spare = padded.shape[1]
    total = parts_ref[0].astype(F32)
    for i in range(1, parts_ref.shape[0]):
        total += parts_ref[i].astype(F32)
    total = total.reshape(slots, wrows // slots, HD)
    zeros = jnp.zeros((spare - wrows // slots, HD), F32)
    for slot in range(slots):
        padded[slot] = jnp.concatenate([total[slot], zeros], axis=0).astype(BF16)
    copy = pltpu.make_async_copy(padded, out_ref.at[:, height - spare : height, :], sem)
    copy.start()
    copy.wait()


def finish(grads, parts, spare):
    return pl.pallas_call(
        finish_kernel,
        out_shape=jax.ShapeDtypeStruct(grads.shape, grads.dtype),
        in_specs=[anywhere(), whole(parts)],
        out_specs=anywhere(),
        scratch_shapes=[pltpu.VMEM((grads.shape[0], spare, HD), BF16), pltpu.SemaphoreType.DMA(())],
        input_output_aliases={0: 0},
        compiler_params=params(),
        cost_estimate=cost(0, 2 * parts.size),
    )(grads, parts)


def slot_of(number, slots):
    even = number % 2 == 0
    distance = number // 2 + 1
    offset = jnp.where(even, slots - distance, distance)
    offset = jnp.where(number == 6, 0, jnp.where(number == 7, 4, offset))
    return lax.rem(lax.axis_index("seq") + offset, slots)


def forward_kernel(rows, length_ref, packed_ref, _, weights_ref, inverse_ref, out_ref, low_ref, value_t, scores_ref):
    slots = packed_ref.shape[0]
    total = slots * rows
    step = pl.program_id(0)

    @pl.when(step == 0)
    def _():
        value_t[...] = packed_ref[:, 2 * rows : 3 * rows, :].reshape(total, HD).T

    keys = packed_ref[:, rows : 2 * rows, :].reshape(total, HD)
    block = jnp.concatenate(
        [packed_ref[slot_of(PAIR * step + i, slots), 0:rows, :] for i in range(PAIR)], axis=0
    )
    scores_ref[...] = lax.dot_general(keys, block, NT, preferred_element_type=F32)
    width = block.shape[0]
    grain = HD
    top = jnp.full((8, width), -jnp.inf, F32)
    for begin in range(0, total, grain):
        bias = jnp.where(begin < length_ref[0], 0.0, -jnp.inf).astype(F32)
        part = scores_ref[begin : begin + grain, :] + bias
        top = jnp.maximum(top, jnp.max(part.reshape(grain // 8, 8, width), axis=0))
    top = jnp.max(top, axis=0, keepdims=True)
    norm = jnp.zeros((8, width), F32)
    for begin in range(0, total, grain):
        bias = jnp.where(begin < length_ref[0], 0.0, -jnp.inf).astype(F32)
        part = jnp.exp2((scores_ref[begin : begin + grain, :] + (bias - top)) * FACTOR_LOG2)
        norm = norm + jnp.sum(part.reshape(grain // 8, 8, width), axis=0)
        weights_ref[begin : begin + grain, :] = part.astype(BF16)
    inverse = 1.0 / jnp.sum(norm, axis=0, keepdims=True)
    inverse_ref[...] = inverse
    weights = weights_ref[...]
    output = jnp.dot(value_t[...], weights, preferred_element_type=F32) * inverse
    out_ref[...] = output
    low_ref[...] = output.astype(BF16)


def attend_forward(packed, lengths, rows, after):
    slots = packed.shape[0]
    total = slots * rows
    width = PAIR * rows
    return pl.pallas_call(
        functools.partial(forward_kernel, rows),
        grid=(slots // PAIR,),
        out_shape=[
            jax.ShapeDtypeStruct((total, total), BF16),
            jax.ShapeDtypeStruct((1, total), F32),
            jax.ShapeDtypeStruct((HD, total), F32),
            jax.ShapeDtypeStruct((HD, total), BF16),
        ],
        in_specs=[smem(), whole(packed), corner(after)],
        out_specs=[
            pl.BlockSpec((total, width), lambda i: (0, i)),
            pl.BlockSpec((1, width), lambda i: (0, i)),
            pl.BlockSpec((HD, width), lambda i: (0, i)),
            pl.BlockSpec((HD, width), lambda i: (0, i)),
        ],
        scratch_shapes=[pltpu.VMEM((HD, total), BF16), pltpu.VMEM((total, width), F32)],
        compiler_params=params(),
        cost_estimate=cost(4 * total * total * HD, 2 * total * total, total * total),
    )(lengths, packed, after)


def project_kernel(*refs):
    *grads, own_weight_ref, other_weight_ref, _, own_ref, other_ref = refs
    half = grads[0].shape[1]
    core = lax.axis_index("tensor")
    mine = pl.ds(pl.multiple_of(core * half, half), half)
    weight = jnp.concatenate([own_weight_ref[mine, :], other_weight_ref[mine, :]], axis=1)
    start = 0
    for grad in grads:
        product = jnp.dot(grad[...], weight, preferred_element_type=F32)
        stop = start + grad.shape[0]
        own_ref[start:stop, :] = product[:, :HD]
        other_ref[start:stop, :] = product[:, HD:].astype(BF16)
        start = stop


def project(grads, own_weight, other_weight, after):
    total = sum(grad.shape[0] for grad in grads)
    features = grads[0].shape[1]
    shapes = [jax.ShapeDtypeStruct((total, HD), F32), jax.ShapeDtypeStruct((total, HD), BF16)]
    return pl.pallas_call(
        project_kernel,
        grid=(1,),
        out_shape=shapes,
        in_specs=[whole(array) for array in (*grads, own_weight, other_weight)] + [corner(after)],
        out_specs=[whole(shape) for shape in shapes],
        compiler_params=params(),
        cost_estimate=cost(4 * total * features * HD, 2 * total * features),
    )(*grads, own_weight, other_weight, after)


def weight_grad_kernel(own_t_ref, other_t_ref, _, *refs):
    *grads, own_ref, other_ref = refs
    outputs = jnp.concatenate([own_t_ref[...], other_t_ref[...]], axis=0)
    for begin in range(0, grads[0].shape[1], FBLOCK):
        columns = slice(begin, begin + FBLOCK)
        grad = jnp.concatenate([grad[:, columns] for grad in grads], axis=0)
        product = jnp.dot(outputs, grad, preferred_element_type=F32).T.astype(BF16)
        own_ref[columns, :] = product[:, :HD]
        other_ref[columns, :] = product[:, HD:]


def weight_grad(own_t, other_t, grads, after):
    rows, features = own_t.shape[1], grads[0].shape[1]
    shapes = [jax.ShapeDtypeStruct((features, HD), BF16)] * 2
    return pl.pallas_call(
        weight_grad_kernel,
        grid=(1,),
        out_shape=shapes,
        in_specs=[whole(own_t), whole(other_t), corner(after)] + [whole(array) for array in grads],
        out_specs=[whole(shape) for shape in shapes],
        compiler_params=params(),
        cost_estimate=cost(4 * rows * features * HD, 2 * rows * features),
    )(own_t, other_t, after, *grads)


def hold_kernel(*refs):
    count = len(refs) // 2
    for source, target in zip(refs[:count], refs[count:]):
        target[...] = source[...]


def hold(arrays, micros):
    return pl.pallas_call(
        hold_kernel,
        out_shape=[jax.ShapeDtypeStruct(array.shape, array.dtype) for array in arrays],
        in_specs=[whole(array) for array in arrays],
        out_specs=[whole(array) for array in arrays],
        compiler_params=params(24),
        cost_estimate=long_cost(micros),
    )(*arrays)


def halves_kernel(left_ref, right_ref, *part_refs):
    half = left_ref.shape[0] // 2
    for ref, parts in ((left_ref, part_refs[:2]), (right_ref, part_refs[2:])):
        parts[0][...] = ref[:half]
        parts[1][...] = ref[half:]


def halves(left, right):
    half, features = left.shape[0] // 2, left.shape[1]
    shape = jax.ShapeDtypeStruct((half, features), BF16)
    return pl.pallas_call(
        halves_kernel,
        out_shape=[shape] * 4,
        in_specs=[whole(left), whole(right)],
        out_specs=[whole(shape)] * 4,
        compiler_params=params(),
        cost_estimate=long_cost(HOLD1),
    )(left, right)


def join_kernel(own_ref, got_ref, _, out_ref, sems):
    core = lax.axis_index("tensor")
    rows = own_ref.shape[0]
    first = pltpu.make_async_copy(own_ref, out_ref.at[pl.ds(core * rows, rows)], sems.at[0])
    second = pltpu.make_async_copy(got_ref, out_ref.at[pl.ds((1 - core) * rows, rows)], sems.at[1])
    first.start()
    second.start()
    first.wait()
    second.wait()


def join(own, got, after):
    return pl.pallas_call(
        join_kernel,
        grid=(1,),
        out_shape=jax.ShapeDtypeStruct((2 * own.shape[0], HD), BF16),
        in_specs=[whole(own), whole(got), corner(after)],
        out_specs=anywhere(),
        scratch_shapes=[pltpu.SemaphoreType.DMA((2,))],
        compiler_params=params(),
        cost_estimate=cost(0, 8 * own.size),
    )(own, got, after)


def backward_kernel(rows, start, first, last, *refs):
    packed_ref, weights_ref, inverse_ref, out_ref, own_ref, got_ref, _, *refs = refs
    slots = packed_ref.shape[0]
    total = slots * rows
    width = PAIR * rows
    step = pl.program_id(0)
    if last:
        *sums, done_ref, result_ref, key_t, query_acc, key_acc, value_acc = refs
    else:
        query_acc, key_acc, value_acc, key_t = refs
    keys = packed_ref[:, rows : 2 * rows, :].reshape(total, HD)

    @pl.when(step == 0)
    def _():
        key_t[...] = keys.T
        key_acc[...] = jnp.zeros_like(key_acc) if first else sums[0][...]
        value_acc[...] = jnp.zeros_like(value_acc) if first else sums[1][...]

    here = pl.ds(pl.multiple_of(step * width, width), width)
    values = packed_ref[:, 2 * rows : 3 * rows, :].reshape(total, HD)
    block = jnp.concatenate(
        [packed_ref[slot_of(start + PAIR * step + i, slots), 0:rows, :] for i in range(PAIR)], axis=0
    )
    grad = (own_ref[...] + got_ref[...].astype(F32)).astype(BF16)
    grad_t = grad.astype(F32).T
    inverse = inverse_ref[...]
    delta = jnp.sum(grad_t * out_ref[...], axis=0, keepdims=True)
    prob_grad = lax.dot_general(values, grad, NT, preferred_element_type=F32)
    weights = weights_ref[...]
    score_grad = (weights.astype(F32) * ((prob_grad - delta) * inverse)).astype(BF16)
    scaled = (grad_t * inverse).T.astype(BF16)
    value_acc[...] += jnp.dot(weights, scaled, preferred_element_type=F32)
    key_acc[...] += jnp.dot(score_grad, block, preferred_element_type=F32)
    query_t = jnp.dot(key_t[...], score_grad, preferred_element_type=F32) * FACTOR
    query_acc[here, :] = query_t.T.astype(BF16)

    if last:

        @pl.when(step == pl.num_programs(0) - 1)
        def _():
            number = 0
            for source in (done_ref, query_acc):
                for place in range(0, source.shape[0], rows):
                    result_ref[slot_of(number, slots), 0:rows, :] = source[place : place + rows, :]
                    number += 1
            result_ref[:, rows : 2 * rows, :] = (
                (key_acc[...] * FACTOR).astype(BF16).reshape(slots, rows, HD)
            )
            result_ref[:, 2 * rows : 3 * rows, :] = (
                value_acc[...].astype(BF16).reshape(slots, rows, HD)
            )


def attend_backward(packed, state, own, got, rows, start, before, after):
    weights, inverse, out = state
    slots = packed.shape[0]
    total = slots * rows
    width = PAIR * rows
    size = own.shape[0]
    first, last = start == 0, start * rows + size == total
    shift = start // PAIR
    sums = [jax.ShapeDtypeStruct((total, HD), F32)] * 2
    if last:
        shapes = [jax.ShapeDtypeStruct(packed.shape, BF16)]
        scratch = [pltpu.VMEM((size, HD), BF16)] + [pltpu.VMEM((total, HD), F32)] * 2
    else:
        shapes = [jax.ShapeDtypeStruct((size, HD), BF16), *sums]
        scratch = []
    return pl.pallas_call(
        functools.partial(backward_kernel, rows, start, first, last),
        grid=(size // width,),
        out_shape=shapes,
        in_specs=[
            whole(packed),
            pl.BlockSpec((total, width), lambda i: (0, i + shift)),
            pl.BlockSpec((1, width), lambda i: (0, i + shift)),
            pl.BlockSpec((HD, width), lambda i: (0, i + shift)),
            pl.BlockSpec((width, HD), lambda i: (i, 0)),
            pl.BlockSpec((width, HD), lambda i: (i, 0)),
            corner(after),
            *[whole(array) for array in before],
        ],
        out_specs=[whole(shape) for shape in shapes],
        scratch_shapes=[pltpu.VMEM((HD, total), BF16), *scratch],
        compiler_params=params(),
        cost_estimate=cost(8 * total * size * HD, 2 * total * size),
    )(packed, weights, inverse, out, own, got, after, *before)


def per_device(queries, keys, values, out_grad, gate, proj_weight, lengths):
    seq, dp = lax.axis_size("seq"), lax.axis_size("dp")
    rows = queries.shape[0]
    wrows = proj_weight.shape[0]
    swap = [(0, 1), (1, 0)]
    right = [(i, (i + 1) % seq) for i in range(seq)]
    left = [(i, (i - 1) % seq) for i in range(seq)]

    def move(array, step):
        return lax.ppermute(array, "seq", right if step > 0 else left)

    own_rows = scale(out_grad, gate, lengths)
    from_left, from_right = move(own_rows, 1), move(own_rows, -1)
    near = [from_left, from_right]
    left_top, left_low, right_top, right_low = halves(from_left, from_right)
    for i in range(2):
        left_top, right_low = move(left_top, 1), move(right_low, -1)
        left_low, right_top = move(left_low, 1), move(right_top, -1)
        if (HOLD2, HOLD3)[i]:
            if i == 0:
                (left_top,) = hold((left_top,), HOLD2)
            else:
                (left_low,) = hold((left_low,), HOLD3)
        near += [left_top, left_low, right_top, right_low]

    packed = lax.all_to_all(
        pack(queries, keys, values, proj_weight, seq), "seq", split_axis=0, concat_axis=0, tiled=True
    )
    weight_rows = packed[:, 3 * rows : 3 * rows + wrows].reshape(1, seq * wrows, HD)
    copies = jnp.broadcast_to(weight_rows, (dp, seq * wrows, HD))
    own_weight = lax.all_to_all(copies, "dp", split_axis=0, concat_axis=0, tiled=True).reshape(-1, HD)
    other_weight = lax.ppermute(own_weight, "tensor", swap)

    *state, low = attend_forward(packed, lengths, rows, copies)
    low_other = lax.ppermute(low, "tensor", swap)

    left_top, right_low, low = lax.optimization_barrier((left_top, right_low, low))
    far = [move(left_top, 1), move(right_low, -1)]
    last = [own_rows, *far]

    near_own, other = project(near, own_weight, other_weight, left_top)
    near_got = lax.ppermute(other, "tensor", swap)
    proj_own, proj_send = weight_grad(low, low_other, [*near, *last], near_own)
    proj_got = lax.ppermute(proj_send, "tensor", swap)
    own, other = project(last, own_weight, other_weight, proj_own)
    got = lax.ppermute(other, "tensor", swap)
    joined = join(proj_own, proj_got, own).reshape(dp, seq * wrows, HD)
    parts = lax.all_to_all(joined, "dp", split_axis=0, concat_axis=0, tiled=True)

    query_rows, *sums = attend_backward(packed, state, near_own, near_got, rows, 0, [], joined)
    grads = attend_backward(packed, state, own, got, rows, 6, [*sums, query_rows], joined)[0]
    result = finish(grads, parts, packed.shape[1] - 3 * rows)
    result = lax.all_to_all(result, "seq", split_axis=0, concat_axis=0, tiled=True)
    return tuple(unpack(result, rows, wrows))


def solution(mesh):
    token = P(("dp", "seq"), "tensor")
    return jax.shard_map(
        per_device,
        mesh=mesh,
        in_specs=(token, token, token, token, P("dp", None), token, P("dp")),
        out_specs=(token, token, token, token),
        check_vma=False,
    )
```

```python
import functools
import math

import jax
import jax.numpy as jnp
from jax import lax
from jax.experimental import pallas as pl
from jax.experimental.pallas import tpu as pltpu
from jax.sharding import PartitionSpec as P

HD = 128
HOLD1, HOLD2, HOLD3, PACK = 100, 100, 100, 24
PAIR = 2
FBLOCK = 256
MIB = 1024 * 1024
BF16 = jnp.bfloat16
F32 = jnp.float32
FACTOR = HD**-0.5
FACTOR_LOG2 = HD**-0.5 * math.log2(math.e)
NT = (((1,), (1,)), ((), ()))


def cost(flops, read, exps=0):
    return pl.CostEstimate(flops=int(flops), bytes_accessed=int(read), transcendentals=int(exps))


def long_cost(micros):
    return cost(micros * 1e9, micros * 3e6)


def params(limit=48):
    return pltpu.CompilerParams(vmem_limit_bytes=limit * MIB)


def whole(array):
    zeros = (0,) * array.ndim
    return pl.BlockSpec(array.shape, lambda *_: zeros)


def smem():
    return pl.BlockSpec(memory_space=pltpu.SMEM)


def scale_kernel(length_ref, grad_ref, gate_ref, out_ref):
    rows, half = grad_ref.shape
    start = pl.multiple_of(lax.axis_index("tensor") * half, HD)
    gate = gate_ref[:, pl.ds(start, half)]
    left = length_ref[0] - lax.axis_index("seq") * rows
    live = lax.broadcasted_iota(jnp.int32, (rows, 1), 0) < left
    out_ref[...] = jnp.where(live, grad_ref[...].astype(F32) * gate, 0.0).astype(BF16)


def scale(out_grad, gate, lengths):
    return pl.pallas_call(
        scale_kernel,
        out_shape=jax.ShapeDtypeStruct(out_grad.shape, BF16),
        in_specs=[smem(), whole(out_grad), whole(gate)],
        out_specs=whole(out_grad),
        compiler_params=params(),
        cost_estimate=cost(0, 4 * out_grad.size),
    )(lengths, out_grad, gate)


def anywhere():
    return pl.BlockSpec(memory_space=pl.ANY)


def corner(array):
    zeros = (0,) * array.ndim
    return pl.BlockSpec((1,) * (array.ndim - 2) + (16, HD), lambda *_: zeros)


def pack_kernel(query_ref, key_ref, value_ref, weight_ref, out_ref):
    rows = query_ref.shape[0]
    slots, height, _ = out_ref.shape
    weight = weight_ref[...].astype(F32)
    spare = height - 3 * rows - weight.shape[0]
    weight = jnp.concatenate([weight, jnp.zeros((spare, weight.shape[1]), F32)], axis=0).astype(BF16)
    for slot in range(slots):
        columns = slice(slot * HD, (slot + 1) * HD)
        for i, ref in enumerate((query_ref, key_ref, value_ref)):
            out_ref[slot, i * rows : (i + 1) * rows, :] = ref[:, columns]
        out_ref[slot, 3 * rows : height, :] = weight[:, columns]


def pack(queries, keys, values, weight, slots):
    rows = queries.shape[0]
    wrows = weight.shape[0]
    shape = jax.ShapeDtypeStruct((slots, 3 * rows + -(-wrows // 16) * 16, HD), BF16)
    return pl.pallas_call(
        pack_kernel,
        out_shape=shape,
        in_specs=[whole(queries), whole(keys), whole(values), whole(weight)],
        out_specs=whole(shape),
        compiler_params=params(PACK),
        cost_estimate=cost(0, 4 * shape.size),
    )(queries, keys, values, weight)


def unpack_kernel(packed_ref, query_ref, key_ref, value_ref, weight_ref, rows_scr, sems):
    rows = query_ref.shape[0]
    slots, height, _ = packed_ref.shape
    copies = []
    for i, ref in enumerate((query_ref, key_ref, value_ref)):
        for slot in range(slots):
            rows_scr[i, :, slot * HD : (slot + 1) * HD] = packed_ref[slot, i * rows : (i + 1) * rows, :]
        copies.append(pltpu.make_async_copy(rows_scr.at[i], ref, sems.at[i]))
        copies[i].start()
    for slot in range(slots):
        last = packed_ref[slot, 3 * rows : height, :].astype(F32)
        weight_ref[:, slot * HD : (slot + 1) * HD] = last[: weight_ref.shape[0]]
    for copy in copies:
        copy.wait()


def unpack(packed, rows, wrows):
    slots = packed.shape[0]
    token = jax.ShapeDtypeStruct((rows, slots * HD), BF16)
    weight = jax.ShapeDtypeStruct((wrows, slots * HD), F32)
    return pl.pallas_call(
        unpack_kernel,
        out_shape=[token, token, token, weight],
        in_specs=[whole(packed)],
        out_specs=[anywhere(), anywhere(), anywhere(), whole(weight)],
        scratch_shapes=[pltpu.VMEM((3, rows, slots * HD), BF16), pltpu.SemaphoreType.DMA((3,))],
        compiler_params=params(),
        cost_estimate=cost(0, 4 * packed.size),
    )(packed)


def finish_kernel(grads_ref, parts_ref, out_ref, padded, sem):
    _, wrows, _ = parts_ref.shape
    slots, height, _ = out_ref.shape
    spare = padded.shape[1]
    total = parts_ref[0].astype(F32)
    for i in range(1, parts_ref.shape[0]):
        total += parts_ref[i].astype(F32)
    total = total.reshape(slots, wrows // slots, HD)
    zeros = jnp.zeros((spare - wrows // slots, HD), F32)
    for slot in range(slots):
        padded[slot] = jnp.concatenate([total[slot], zeros], axis=0).astype(BF16)
    copy = pltpu.make_async_copy(padded, out_ref.at[:, height - spare : height, :], sem)
    copy.start()
    copy.wait()


def finish(grads, parts, spare):
    return pl.pallas_call(
        finish_kernel,
        out_shape=jax.ShapeDtypeStruct(grads.shape, grads.dtype),
        in_specs=[anywhere(), whole(parts)],
        out_specs=anywhere(),
        scratch_shapes=[pltpu.VMEM((grads.shape[0], spare, HD), BF16), pltpu.SemaphoreType.DMA(())],
        input_output_aliases={0: 0},
        compiler_params=params(),
        cost_estimate=cost(0, 2 * parts.size),
    )(grads, parts)


def spread_kernel(rows, wrows, packed_ref, _, out_ref, weight_scr):
    slots, height, _ = packed_ref.shape
    for slot in range(slots):
        last = packed_ref[slot, 3 * rows : height, :].astype(F32)
        weight_scr[slot * wrows : (slot + 1) * wrows, :] = last[:wrows]
    out_ref[...] = jnp.broadcast_to(weight_scr[...].astype(BF16)[None], out_ref.shape)


def spread(packed, rows, wrows, copies, after):
    total = packed.shape[0] * wrows
    shape = jax.ShapeDtypeStruct((copies, total, HD), BF16)
    return pl.pallas_call(
        functools.partial(spread_kernel, rows, wrows),
        grid=(1,),
        out_shape=shape,
        in_specs=[whole(packed), corner(after)],
        out_specs=whole(shape),
        scratch_shapes=[pltpu.VMEM((total, HD), F32)],
        compiler_params=params(),
        cost_estimate=cost(0, 2 * shape.size),
    )(packed, after)


def slot_of(number, slots):
    even = number % 2 == 0
    distance = number // 2 + 1
    offset = jnp.where(even, slots - distance, distance)
    offset = jnp.where(number == 6, 0, jnp.where(number == 7, 4, offset))
    return lax.rem(lax.axis_index("seq") + offset, slots)


def forward_kernel(rows, length_ref, packed_ref, _, weights_ref, inverse_ref, out_ref, low_ref, value_t, scores_ref):
    slots = packed_ref.shape[0]
    total = slots * rows
    step = pl.program_id(0)

    @pl.when(step == 0)
    def _():
        value_t[...] = packed_ref[:, 2 * rows : 3 * rows, :].reshape(total, HD).T

    keys = packed_ref[:, rows : 2 * rows, :].reshape(total, HD)
    block = jnp.concatenate(
        [packed_ref[slot_of(PAIR * step + i, slots), 0:rows, :] for i in range(PAIR)], axis=0
    )
    scores_ref[...] = lax.dot_general(keys, block, NT, preferred_element_type=F32)
    width = block.shape[0]
    grain = HD
    top = jnp.full((8, width), -jnp.inf, F32)
    for begin in range(0, total, grain):
        bias = jnp.where(begin < length_ref[0], 0.0, -jnp.inf).astype(F32)
        part = scores_ref[begin : begin + grain, :]
        top = jnp.maximum(top, jnp.max(part.reshape(grain // 8, 8, width), axis=0) + bias)
    top = jnp.max(top, axis=0, keepdims=True)
    norm = jnp.zeros((8, width), F32)
    for begin in range(0, total, grain):
        bias = jnp.where(begin < length_ref[0], 0.0, -jnp.inf).astype(F32)
        part = jnp.exp2((scores_ref[begin : begin + grain, :] + (bias - top)) * FACTOR_LOG2)
        norm = norm + jnp.sum(part.reshape(grain // 8, 8, width), axis=0)
        weights_ref[begin : begin + grain, :] = part.astype(BF16)
    inverse = 1.0 / jnp.sum(norm, axis=0, keepdims=True)
    inverse_ref[...] = inverse
    weights = weights_ref[...]
    output = jnp.dot(value_t[...], weights, preferred_element_type=F32) * inverse
    out_ref[...] = output
    low_ref[...] = output.astype(BF16)


def attend_forward(packed, lengths, rows, after):
    slots = packed.shape[0]
    total = slots * rows
    width = PAIR * rows
    return pl.pallas_call(
        functools.partial(forward_kernel, rows),
        grid=(slots // PAIR,),
        out_shape=[
            jax.ShapeDtypeStruct((total, total), BF16),
            jax.ShapeDtypeStruct((1, total), F32),
            jax.ShapeDtypeStruct((HD, total), F32),
            jax.ShapeDtypeStruct((HD, total), BF16),
        ],
        in_specs=[smem(), whole(packed), corner(after)],
        out_specs=[
            pl.BlockSpec((total, width), lambda i: (0, i)),
            pl.BlockSpec((1, width), lambda i: (0, i)),
            pl.BlockSpec((HD, width), lambda i: (0, i)),
            pl.BlockSpec((HD, width), lambda i: (0, i)),
        ],
        scratch_shapes=[pltpu.VMEM((HD, total), BF16), pltpu.VMEM((total, width), F32)],
        compiler_params=params(),
        cost_estimate=cost(4 * total * total * HD, 2 * total * total, total * total),
    )(lengths, packed, after)


def project_kernel(*refs):
    *grads, own_weight_ref, other_weight_ref, _, own_ref, other_ref = refs
    half = grads[0].shape[1]
    core = lax.axis_index("tensor")
    mine = pl.ds(pl.multiple_of(core * half, half), half)
    weight = jnp.concatenate([own_weight_ref[mine, :], other_weight_ref[mine, :]], axis=1)
    start = 0
    for grad in grads:
        product = jnp.dot(grad[...], weight, preferred_element_type=F32)
        stop = start + grad.shape[0]
        own_ref[start:stop, :] = product[:, :HD]
        other_ref[start:stop, :] = product[:, HD:].astype(BF16)
        start = stop


def project(grads, own_weight, other_weight, after):
    total = sum(grad.shape[0] for grad in grads)
    features = grads[0].shape[1]
    shapes = [jax.ShapeDtypeStruct((total, HD), F32), jax.ShapeDtypeStruct((total, HD), BF16)]
    return pl.pallas_call(
        project_kernel,
        grid=(1,),
        out_shape=shapes,
        in_specs=[whole(array) for array in (*grads, own_weight, other_weight)] + [corner(after)],
        out_specs=[whole(shape) for shape in shapes],
        compiler_params=params(),
        cost_estimate=cost(4 * total * features * HD, 2 * total * features),
    )(*grads, own_weight, other_weight, after)


def weight_grad_kernel(own_t_ref, other_t_ref, _, *refs):
    *grads, own_ref, other_ref = refs
    outputs = jnp.concatenate([own_t_ref[...], other_t_ref[...]], axis=0)
    for begin in range(0, grads[0].shape[1], FBLOCK):
        columns = slice(begin, begin + FBLOCK)
        grad = jnp.concatenate([grad[:, columns] for grad in grads], axis=0)
        product = jnp.dot(outputs, grad, preferred_element_type=F32).T.astype(BF16)
        own_ref[columns, :] = product[:, :HD]
        other_ref[columns, :] = product[:, HD:]


def weight_grad(own_t, other_t, grads, after):
    rows, features = own_t.shape[1], grads[0].shape[1]
    shapes = [jax.ShapeDtypeStruct((features, HD), BF16)] * 2
    return pl.pallas_call(
        weight_grad_kernel,
        grid=(1,),
        out_shape=shapes,
        in_specs=[whole(own_t), whole(other_t), corner(after)] + [whole(array) for array in grads],
        out_specs=[whole(shape) for shape in shapes],
        compiler_params=params(),
        cost_estimate=cost(4 * rows * features * HD, 2 * rows * features),
    )(own_t, other_t, after, *grads)


def hold_kernel(*refs):
    count = len(refs) // 2
    for source, target in zip(refs[:count], refs[count:]):
        target[...] = source[...]


def hold(arrays, micros):
    return pl.pallas_call(
        hold_kernel,
        out_shape=[jax.ShapeDtypeStruct(array.shape, array.dtype) for array in arrays],
        in_specs=[whole(array) for array in arrays],
        out_specs=[whole(array) for array in arrays],
        compiler_params=params(24),
        cost_estimate=long_cost(micros),
    )(*arrays)


def halves_kernel(left_ref, right_ref, *part_refs):
    half = left_ref.shape[0] // 2
    for ref, parts in ((left_ref, part_refs[:2]), (right_ref, part_refs[2:])):
        parts[0][...] = ref[:half]
        parts[1][...] = ref[half:]


def halves(left, right):
    half, features = left.shape[0] // 2, left.shape[1]
    shape = jax.ShapeDtypeStruct((half, features), BF16)
    return pl.pallas_call(
        halves_kernel,
        out_shape=[shape] * 4,
        in_specs=[whole(left), whole(right)],
        out_specs=[whole(shape)] * 4,
        compiler_params=params(),
        cost_estimate=long_cost(HOLD1),
    )(left, right)


def join_kernel(own_ref, got_ref, _, out_ref, sems):
    core = lax.axis_index("tensor")
    rows = own_ref.shape[0]
    first = pltpu.make_async_copy(own_ref, out_ref.at[pl.ds(core * rows, rows)], sems.at[0])
    second = pltpu.make_async_copy(got_ref, out_ref.at[pl.ds((1 - core) * rows, rows)], sems.at[1])
    first.start()
    second.start()
    first.wait()
    second.wait()


def join(own, got, after):
    return pl.pallas_call(
        join_kernel,
        grid=(1,),
        out_shape=jax.ShapeDtypeStruct((2 * own.shape[0], HD), BF16),
        in_specs=[anywhere(), anywhere(), corner(after)],
        out_specs=anywhere(),
        scratch_shapes=[pltpu.SemaphoreType.DMA((2,))],
        compiler_params=params(),
        cost_estimate=cost(0, 8 * own.size),
    )(own, got, after)


def backward_kernel(rows, start, first, last, *refs):
    packed_ref, weights_ref, inverse_ref, out_ref, own_ref, got_ref, _, *refs = refs
    slots = packed_ref.shape[0]
    total = slots * rows
    width = PAIR * rows
    step = pl.program_id(0)
    if last:
        *sums, done_ref, result_ref, key_t, query_acc, key_acc, value_acc = refs
    else:
        query_acc, key_acc, value_acc, key_t = refs
    keys = packed_ref[:, rows : 2 * rows, :].reshape(total, HD)

    @pl.when(step == 0)
    def _():
        key_t[...] = keys.T
        key_acc[...] = jnp.zeros_like(key_acc) if first else sums[0][...]
        value_acc[...] = jnp.zeros_like(value_acc) if first else sums[1][...]

    here = pl.ds(pl.multiple_of(step * width, width), width)
    values = packed_ref[:, 2 * rows : 3 * rows, :].reshape(total, HD)
    block = jnp.concatenate(
        [packed_ref[slot_of(start + PAIR * step + i, slots), 0:rows, :] for i in range(PAIR)], axis=0
    )
    grad = (own_ref[...] + got_ref[...].astype(F32)).astype(BF16)
    grad_t = grad.astype(F32).T
    inverse = inverse_ref[...]
    delta = jnp.sum(grad_t * out_ref[...], axis=0, keepdims=True)
    prob_grad = lax.dot_general(values, grad, NT, preferred_element_type=F32)
    weights = weights_ref[...]
    score_grad = (weights.astype(F32) * ((prob_grad - delta) * inverse)).astype(BF16)
    scaled = (grad_t * inverse).T.astype(BF16)
    value_acc[...] += jnp.dot(weights, scaled, preferred_element_type=F32)
    key_acc[...] += jnp.dot(score_grad, block, preferred_element_type=F32)
    query_t = jnp.dot(key_t[...], score_grad, preferred_element_type=F32) * FACTOR
    query_acc[here, :] = query_t.T.astype(BF16)

    if last:

        @pl.when(step == pl.num_programs(0) - 1)
        def _():
            number = 0
            for source in (done_ref, query_acc):
                for place in range(0, source.shape[0], rows):
                    result_ref[slot_of(number, slots), 0:rows, :] = source[place : place + rows, :]
                    number += 1
            result_ref[:, rows : 2 * rows, :] = (
                (key_acc[...] * FACTOR).astype(BF16).reshape(slots, rows, HD)
            )
            result_ref[:, 2 * rows : 3 * rows, :] = (
                value_acc[...].astype(BF16).reshape(slots, rows, HD)
            )


def attend_backward(packed, state, own, got, rows, start, before, after):
    weights, inverse, out = state
    slots = packed.shape[0]
    total = slots * rows
    width = PAIR * rows
    size = own.shape[0]
    first, last = start == 0, start * rows + size == total
    shift = start // PAIR
    sums = [jax.ShapeDtypeStruct((total, HD), F32)] * 2
    if last:
        shapes = [jax.ShapeDtypeStruct(packed.shape, BF16)]
        scratch = [pltpu.VMEM((size, HD), BF16)] + [pltpu.VMEM((total, HD), F32)] * 2
    else:
        shapes = [jax.ShapeDtypeStruct((size, HD), BF16), *sums]
        scratch = []
    return pl.pallas_call(
        functools.partial(backward_kernel, rows, start, first, last),
        grid=(size // width,),
        out_shape=shapes,
        in_specs=[
            whole(packed),
            pl.BlockSpec((total, width), lambda i: (0, i + shift)),
            pl.BlockSpec((1, width), lambda i: (0, i + shift)),
            pl.BlockSpec((HD, width), lambda i: (0, i + shift)),
            pl.BlockSpec((width, HD), lambda i: (i, 0)),
            pl.BlockSpec((width, HD), lambda i: (i, 0)),
            corner(after),
            *[whole(array) for array in before],
        ],
        out_specs=[whole(shape) for shape in shapes],
        scratch_shapes=[pltpu.VMEM((HD, total), BF16), *scratch],
        compiler_params=params(),
        cost_estimate=cost(8 * total * size * HD, 2 * total * size),
    )(packed, weights, inverse, out, own, got, after, *before)


def per_device(queries, keys, values, out_grad, gate, proj_weight, lengths):
    seq, dp = lax.axis_size("seq"), lax.axis_size("dp")
    rows = queries.shape[0]
    wrows = proj_weight.shape[0]
    swap = [(0, 1), (1, 0)]
    right = [(i, (i + 1) % seq) for i in range(seq)]
    left = [(i, (i - 1) % seq) for i in range(seq)]

    def move(array, step):
        return lax.ppermute(array, "seq", right if step > 0 else left)

    own_rows = scale(out_grad, gate, lengths)
    from_left, from_right = move(own_rows, 1), move(own_rows, -1)
    near = [from_left, from_right]
    left_top, left_low, right_top, right_low = halves(from_left, from_right)
    for i in range(2):
        left_top, right_low = move(left_top, 1), move(right_low, -1)
        left_low, right_top = move(left_low, 1), move(right_top, -1)
        if (HOLD2, HOLD3)[i]:
            if i == 0:
                (left_top,) = hold((left_top,), HOLD2)
            else:
                (left_low,) = hold((left_low,), HOLD3)
        near += [left_top, left_low, right_top, right_low]

    packed = lax.all_to_all(
        pack(queries, keys, values, proj_weight, seq), "seq", split_axis=0, concat_axis=0, tiled=True
    )
    copies = spread(packed, rows, wrows, dp, packed)
    own_weight = lax.all_to_all(copies, "dp", split_axis=0, concat_axis=0, tiled=True).reshape(-1, HD)
    other_weight = lax.ppermute(own_weight, "tensor", swap)

    *state, low = attend_forward(packed, lengths, rows, copies)
    low_other = lax.ppermute(low, "tensor", swap)

    left_top, right_low, low = lax.optimization_barrier((left_top, right_low, low))
    far = [move(left_top, 1), move(right_low, -1)]
    last = [own_rows, *far]

    near_own, other = project(near, own_weight, other_weight, left_top)
    near_got = lax.ppermute(other, "tensor", swap)
    proj_own, proj_send = weight_grad(low, low_other, [*near, *last], near_own)
    proj_got = lax.ppermute(proj_send, "tensor", swap)
    own, other = project(last, own_weight, other_weight, proj_own)
    got = lax.ppermute(other, "tensor", swap)
    joined = join(proj_own, proj_got, own).reshape(dp, seq * wrows, HD)
    parts = lax.all_to_all(joined, "dp", split_axis=0, concat_axis=0, tiled=True)

    query_rows, *sums = attend_backward(packed, state, near_own, near_got, rows, 0, [], joined)
    grads = attend_backward(packed, state, own, got, rows, 6, [*sums, query_rows], joined)[0]
    result = finish(grads, parts, packed.shape[1] - 3 * rows)
    result = lax.all_to_all(result, "seq", split_axis=0, concat_axis=0, tiled=True)
    return tuple(unpack(result, rows, wrows))


def solution(mesh):
    token = P(("dp", "seq"), "tensor")
    return jax.shard_map(
        per_device,
        mesh=mesh,
        in_specs=(token, token, token, token, P("dp", None), token, P("dp")),
        out_specs=(token, token, token, token),
        check_vma=False,
    )
```

```python
import functools
import math

import jax
import jax.numpy as jnp
from jax import lax
from jax.experimental import pallas as pl
from jax.experimental.pallas import tpu as pltpu
from jax.sharding import PartitionSpec as P

HD = 128
HOLD1, HOLD2, HOLD3, PACK = 100, 100, 100, 24
PAIR = 2
WIDE = 4
FBLOCK = 256
MIB = 1024 * 1024
BF16 = jnp.bfloat16
F32 = jnp.float32
FACTOR = HD**-0.5
FACTOR_LOG2 = HD**-0.5 * math.log2(math.e)
NT = (((1,), (1,)), ((), ()))


def cost(flops, read, exps=0):
    return pl.CostEstimate(flops=int(flops), bytes_accessed=int(read), transcendentals=int(exps))


def long_cost(micros):
    return cost(micros * 1e9, micros * 3e6)


def params(limit=48):
    return pltpu.CompilerParams(vmem_limit_bytes=limit * MIB)


def whole(array):
    zeros = (0,) * array.ndim
    return pl.BlockSpec(array.shape, lambda *_: zeros)


def smem():
    return pl.BlockSpec(memory_space=pltpu.SMEM)


def scale_kernel(length_ref, grad_ref, gate_ref, out_ref):
    rows, half = grad_ref.shape
    start = pl.multiple_of(lax.axis_index("tensor") * half, HD)
    gate = gate_ref[:, pl.ds(start, half)]
    left = length_ref[0] - lax.axis_index("seq") * rows
    live = lax.broadcasted_iota(jnp.int32, (rows, 1), 0) < left
    out_ref[...] = jnp.where(live, grad_ref[...].astype(F32) * gate, 0.0).astype(BF16)


def scale(out_grad, gate, lengths):
    return pl.pallas_call(
        scale_kernel,
        out_shape=jax.ShapeDtypeStruct(out_grad.shape, BF16),
        in_specs=[smem(), whole(out_grad), whole(gate)],
        out_specs=whole(out_grad),
        compiler_params=params(),
        cost_estimate=cost(0, 4 * out_grad.size),
    )(lengths, out_grad, gate)


def anywhere():
    return pl.BlockSpec(memory_space=pl.ANY)


def corner(array):
    zeros = (0,) * array.ndim
    return pl.BlockSpec((1,) * (array.ndim - 2) + (16, HD), lambda *_: zeros)


def pack_kernel(query_ref, key_ref, value_ref, weight_ref, out_ref):
    rows = query_ref.shape[0]
    slots, height, _ = out_ref.shape
    weight = weight_ref[...].astype(F32)
    spare = height - 3 * rows - weight.shape[0]
    weight = jnp.concatenate([weight, jnp.zeros((spare, weight.shape[1]), F32)], axis=0).astype(BF16)
    for slot in range(slots):
        columns = slice(slot * HD, (slot + 1) * HD)
        for i, ref in enumerate((query_ref, key_ref, value_ref)):
            out_ref[slot, i * rows : (i + 1) * rows, :] = ref[:, columns]
        out_ref[slot, 3 * rows : height, :] = weight[:, columns]


def pack(queries, keys, values, weight, slots):
    rows = queries.shape[0]
    wrows = weight.shape[0]
    shape = jax.ShapeDtypeStruct((slots, 3 * rows + -(-wrows // 16) * 16, HD), BF16)
    return pl.pallas_call(
        pack_kernel,
        out_shape=shape,
        in_specs=[whole(queries), whole(keys), whole(values), whole(weight)],
        out_specs=whole(shape),
        compiler_params=params(PACK),
        cost_estimate=cost(0, 4 * shape.size),
    )(queries, keys, values, weight)


def unpack_kernel(packed_ref, query_ref, key_ref, value_ref, weight_ref, rows_scr, sems):
    rows = query_ref.shape[0]
    slots, height, _ = packed_ref.shape
    copies = []
    for i, ref in enumerate((query_ref, key_ref, value_ref)):
        for slot in range(slots):
            rows_scr[i, :, slot * HD : (slot + 1) * HD] = packed_ref[slot, i * rows : (i + 1) * rows, :]
        copies.append(pltpu.make_async_copy(rows_scr.at[i], ref, sems.at[i]))
        copies[i].start()
    for slot in range(slots):
        last = packed_ref[slot, 3 * rows : height, :].astype(F32)
        weight_ref[:, slot * HD : (slot + 1) * HD] = last[: weight_ref.shape[0]]
    for copy in copies:
        copy.wait()


def unpack(packed, rows, wrows):
    slots = packed.shape[0]
    token = jax.ShapeDtypeStruct((rows, slots * HD), BF16)
    weight = jax.ShapeDtypeStruct((wrows, slots * HD), F32)
    return pl.pallas_call(
        unpack_kernel,
        out_shape=[token, token, token, weight],
        in_specs=[whole(packed)],
        out_specs=[anywhere(), anywhere(), anywhere(), whole(weight)],
        scratch_shapes=[pltpu.VMEM((3, rows, slots * HD), BF16), pltpu.SemaphoreType.DMA((3,))],
        compiler_params=params(),
        cost_estimate=cost(0, 4 * packed.size),
    )(packed)


def finish_kernel(grads_ref, parts_ref, out_ref, padded, sem):
    _, wrows, _ = parts_ref.shape
    slots, height, _ = out_ref.shape
    spare = padded.shape[1]
    total = parts_ref[0].astype(F32)
    for i in range(1, parts_ref.shape[0]):
        total += parts_ref[i].astype(F32)
    total = total.reshape(slots, wrows // slots, HD)
    zeros = jnp.zeros((spare - wrows // slots, HD), F32)
    for slot in range(slots):
        padded[slot] = jnp.concatenate([total[slot], zeros], axis=0).astype(BF16)
    copy = pltpu.make_async_copy(padded, out_ref.at[:, height - spare : height, :], sem)
    copy.start()
    copy.wait()


def finish(grads, parts, spare):
    return pl.pallas_call(
        finish_kernel,
        out_shape=jax.ShapeDtypeStruct(grads.shape, grads.dtype),
        in_specs=[anywhere(), whole(parts)],
        out_specs=anywhere(),
        scratch_shapes=[pltpu.VMEM((grads.shape[0], spare, HD), BF16), pltpu.SemaphoreType.DMA(())],
        input_output_aliases={0: 0},
        compiler_params=params(),
        cost_estimate=cost(0, 2 * parts.size),
    )(grads, parts)


def spread_kernel(rows, wrows, packed_ref, _, out_ref, weight_scr):
    slots, height, _ = packed_ref.shape
    for slot in range(slots):
        last = packed_ref[slot, 3 * rows : height, :].astype(F32)
        weight_scr[slot * wrows : (slot + 1) * wrows, :] = last[:wrows]
    out_ref[...] = jnp.broadcast_to(weight_scr[...].astype(BF16)[None], out_ref.shape)


def spread(packed, rows, wrows, copies, after):
    total = packed.shape[0] * wrows
    shape = jax.ShapeDtypeStruct((copies, total, HD), BF16)
    return pl.pallas_call(
        functools.partial(spread_kernel, rows, wrows),
        grid=(1,),
        out_shape=shape,
        in_specs=[whole(packed), corner(after)],
        out_specs=whole(shape),
        scratch_shapes=[pltpu.VMEM((total, HD), F32)],
        compiler_params=params(),
        cost_estimate=cost(0, 2 * shape.size),
    )(packed, after)


def slot_of(number, slots):
    even = number % 2 == 0
    distance = number // 2 + 1
    offset = jnp.where(even, slots - distance, distance)
    offset = jnp.where(number == 6, 0, jnp.where(number == 7, 4, offset))
    return lax.rem(lax.axis_index("seq") + offset, slots)


def forward_kernel(rows, length_ref, packed_ref, _, weights_ref, inverse_ref, out_ref, low_ref, value_t, scores_ref):
    slots = packed_ref.shape[0]
    total = slots * rows
    step = pl.program_id(0)

    @pl.when(step == 0)
    def _():
        value_t[...] = packed_ref[:, 2 * rows : 3 * rows, :].reshape(total, HD).T

    keys = packed_ref[:, rows : 2 * rows, :].reshape(total, HD)
    block = jnp.concatenate(
        [packed_ref[slot_of(WIDE * step + i, slots), 0:rows, :] for i in range(WIDE)], axis=0
    )
    scores_ref[...] = lax.dot_general(keys, block, NT, preferred_element_type=F32)
    width = block.shape[0]
    grain = HD
    top = jnp.full((8, width), -jnp.inf, F32)
    for begin in range(0, total, grain):
        bias = jnp.where(begin < length_ref[0], 0.0, -jnp.inf).astype(F32)
        part = scores_ref[begin : begin + grain, :]
        top = jnp.maximum(top, jnp.max(part.reshape(grain // 8, 8, width), axis=0) + bias)
    top = jnp.max(top, axis=0, keepdims=True)
    norm = jnp.zeros((8, width), F32)
    for begin in range(0, total, grain):
        bias = jnp.where(begin < length_ref[0], 0.0, -jnp.inf).astype(F32)
        part = jnp.exp2((scores_ref[begin : begin + grain, :] + (bias - top)) * FACTOR_LOG2)
        norm = norm + jnp.sum(part.reshape(grain // 8, 8, width), axis=0)
        weights_ref[begin : begin + grain, :] = part.astype(BF16)
    inverse = 1.0 / jnp.sum(norm, axis=0, keepdims=True)
    inverse_ref[...] = inverse
    weights = weights_ref[...]
    output = jnp.dot(value_t[...], weights, preferred_element_type=F32) * inverse
    out_ref[...] = output
    low_ref[...] = output.astype(BF16)


def attend_forward(packed, lengths, rows, after):
    slots = packed.shape[0]
    total = slots * rows
    width = WIDE * rows
    return pl.pallas_call(
        functools.partial(forward_kernel, rows),
        grid=(slots // WIDE,),
        out_shape=[
            jax.ShapeDtypeStruct((total, total), BF16),
            jax.ShapeDtypeStruct((1, total), F32),
            jax.ShapeDtypeStruct((HD, total), F32),
            jax.ShapeDtypeStruct((HD, total), BF16),
        ],
        in_specs=[smem(), whole(packed), corner(after)],
        out_specs=[
            pl.BlockSpec((total, width), lambda i: (0, i)),
            pl.BlockSpec((1, width), lambda i: (0, i)),
            pl.BlockSpec((HD, width), lambda i: (0, i)),
            pl.BlockSpec((HD, width), lambda i: (0, i)),
        ],
        scratch_shapes=[pltpu.VMEM((HD, total), BF16), pltpu.VMEM((total, width), F32)],
        compiler_params=params(),
        cost_estimate=cost(4 * total * total * HD, 2 * total * total, total * total),
    )(lengths, packed, after)


def project_kernel(*refs):
    *grads, own_weight_ref, other_weight_ref, _, own_ref, other_ref = refs
    half = grads[0].shape[1]
    core = lax.axis_index("tensor")
    mine = pl.ds(pl.multiple_of(core * half, half), half)
    weight = jnp.concatenate([own_weight_ref[mine, :], other_weight_ref[mine, :]], axis=1)
    start = 0
    for grad in grads:
        product = jnp.dot(grad[...], weight, preferred_element_type=F32)
        stop = start + grad.shape[0]
        own_ref[start:stop, :] = product[:, :HD]
        other_ref[start:stop, :] = product[:, HD:].astype(BF16)
        start = stop


def project(grads, own_weight, other_weight, after):
    total = sum(grad.shape[0] for grad in grads)
    features = grads[0].shape[1]
    shapes = [jax.ShapeDtypeStruct((total, HD), F32), jax.ShapeDtypeStruct((total, HD), BF16)]
    return pl.pallas_call(
        project_kernel,
        grid=(1,),
        out_shape=shapes,
        in_specs=[whole(array) for array in (*grads, own_weight, other_weight)] + [corner(after)],
        out_specs=[whole(shape) for shape in shapes],
        compiler_params=params(),
        cost_estimate=cost(4 * total * features * HD, 2 * total * features),
    )(*grads, own_weight, other_weight, after)


def weight_grad_kernel(own_t_ref, other_t_ref, _, *refs):
    *grads, own_ref, other_ref = refs
    outputs = jnp.concatenate([own_t_ref[...], other_t_ref[...]], axis=0)
    for begin in range(0, grads[0].shape[1], FBLOCK):
        columns = slice(begin, begin + FBLOCK)
        grad = jnp.concatenate([grad[:, columns] for grad in grads], axis=0)
        product = jnp.dot(outputs, grad, preferred_element_type=F32).T.astype(BF16)
        own_ref[columns, :] = product[:, :HD]
        other_ref[columns, :] = product[:, HD:]


def weight_grad(own_t, other_t, grads, after):
    rows, features = own_t.shape[1], grads[0].shape[1]
    shapes = [jax.ShapeDtypeStruct((features, HD), BF16)] * 2
    return pl.pallas_call(
        weight_grad_kernel,
        grid=(1,),
        out_shape=shapes,
        in_specs=[whole(own_t), whole(other_t), corner(after)] + [whole(array) for array in grads],
        out_specs=[whole(shape) for shape in shapes],
        compiler_params=params(),
        cost_estimate=cost(4 * rows * features * HD, 2 * rows * features),
    )(own_t, other_t, after, *grads)


def hold_kernel(*refs):
    count = len(refs) // 2
    for source, target in zip(refs[:count], refs[count:]):
        target[...] = source[...]


def hold(arrays, micros):
    return pl.pallas_call(
        hold_kernel,
        out_shape=[jax.ShapeDtypeStruct(array.shape, array.dtype) for array in arrays],
        in_specs=[whole(array) for array in arrays],
        out_specs=[whole(array) for array in arrays],
        compiler_params=params(24),
        cost_estimate=long_cost(micros),
    )(*arrays)


def halves_kernel(left_ref, right_ref, *part_refs):
    half = left_ref.shape[0] // 2
    for ref, parts in ((left_ref, part_refs[:2]), (right_ref, part_refs[2:])):
        parts[0][...] = ref[:half]
        parts[1][...] = ref[half:]


def halves(left, right):
    half, features = left.shape[0] // 2, left.shape[1]
    shape = jax.ShapeDtypeStruct((half, features), BF16)
    return pl.pallas_call(
        halves_kernel,
        out_shape=[shape] * 4,
        in_specs=[whole(left), whole(right)],
        out_specs=[whole(shape)] * 4,
        compiler_params=params(),
        cost_estimate=long_cost(HOLD1),
    )(left, right)


def join_kernel(own_ref, got_ref, _, out_ref, sems):
    core = lax.axis_index("tensor")
    rows = own_ref.shape[0]
    first = pltpu.make_async_copy(own_ref, out_ref.at[pl.ds(core * rows, rows)], sems.at[0])
    second = pltpu.make_async_copy(got_ref, out_ref.at[pl.ds((1 - core) * rows, rows)], sems.at[1])
    first.start()
    second.start()
    first.wait()
    second.wait()


def join(own, got, after):
    return pl.pallas_call(
        join_kernel,
        grid=(1,),
        out_shape=jax.ShapeDtypeStruct((2 * own.shape[0], HD), BF16),
        in_specs=[anywhere(), anywhere(), corner(after)],
        out_specs=anywhere(),
        scratch_shapes=[pltpu.SemaphoreType.DMA((2,))],
        compiler_params=params(),
        cost_estimate=cost(0, 8 * own.size),
    )(own, got, after)


def backward_kernel(rows, start, first, last, *refs):
    packed_ref, weights_ref, inverse_ref, out_ref, own_ref, got_ref, _, *refs = refs
    slots = packed_ref.shape[0]
    total = slots * rows
    width = PAIR * rows
    step = pl.program_id(0)
    if last:
        *sums, done_ref, result_ref, key_t, query_acc, key_acc, value_acc = refs
    else:
        query_acc, key_acc, value_acc, key_t = refs
    keys = packed_ref[:, rows : 2 * rows, :].reshape(total, HD)

    @pl.when(step == 0)
    def _():
        key_t[...] = keys.T
        key_acc[...] = jnp.zeros_like(key_acc) if first else sums[0][...]
        value_acc[...] = jnp.zeros_like(value_acc) if first else sums[1][...]

    here = pl.ds(pl.multiple_of(step * width, width), width)
    values = packed_ref[:, 2 * rows : 3 * rows, :].reshape(total, HD)
    block = jnp.concatenate(
        [packed_ref[slot_of(start + PAIR * step + i, slots), 0:rows, :] for i in range(PAIR)], axis=0
    )
    grad = (own_ref[...] + got_ref[...].astype(F32)).astype(BF16)
    grad_t = grad.astype(F32).T
    inverse = inverse_ref[...]
    delta = jnp.sum(grad_t * out_ref[...], axis=0, keepdims=True)
    prob_grad = lax.dot_general(values, grad, NT, preferred_element_type=F32)
    weights = weights_ref[...]
    score_grad = (weights.astype(F32) * ((prob_grad - delta) * inverse)).astype(BF16)
    scaled = (grad_t * inverse).T.astype(BF16)
    value_acc[...] += jnp.dot(weights, scaled, preferred_element_type=F32)
    key_acc[...] += jnp.dot(score_grad, block, preferred_element_type=F32)
    query_t = jnp.dot(key_t[...], score_grad, preferred_element_type=F32) * FACTOR
    query_acc[here, :] = query_t.T.astype(BF16)

    if last:

        @pl.when(step == pl.num_programs(0) - 1)
        def _():
            number = 0
            for source in (done_ref, query_acc):
                for place in range(0, source.shape[0], rows):
                    result_ref[slot_of(number, slots), 0:rows, :] = source[place : place + rows, :]
                    number += 1
            result_ref[:, rows : 2 * rows, :] = (
                (key_acc[...] * FACTOR).astype(BF16).reshape(slots, rows, HD)
            )
            result_ref[:, 2 * rows : 3 * rows, :] = (
                value_acc[...].astype(BF16).reshape(slots, rows, HD)
            )


def attend_backward(packed, state, own, got, rows, start, before, after):
    weights, inverse, out = state
    slots = packed.shape[0]
    total = slots * rows
    width = PAIR * rows
    size = own.shape[0]
    first, last = start == 0, start * rows + size == total
    shift = start // PAIR
    sums = [jax.ShapeDtypeStruct((total, HD), F32)] * 2
    if last:
        shapes = [jax.ShapeDtypeStruct(packed.shape, BF16)]
        scratch = [pltpu.VMEM((size, HD), BF16)] + [pltpu.VMEM((total, HD), F32)] * 2
    else:
        shapes = [jax.ShapeDtypeStruct((size, HD), BF16), *sums]
        scratch = []
    return pl.pallas_call(
        functools.partial(backward_kernel, rows, start, first, last),
        grid=(size // width,),
        out_shape=shapes,
        in_specs=[
            whole(packed),
            pl.BlockSpec((total, width), lambda i: (0, i + shift)),
            pl.BlockSpec((1, width), lambda i: (0, i + shift)),
            pl.BlockSpec((HD, width), lambda i: (0, i + shift)),
            pl.BlockSpec((width, HD), lambda i: (i, 0)),
            pl.BlockSpec((width, HD), lambda i: (i, 0)),
            corner(after),
            *[whole(array) for array in before],
        ],
        out_specs=[whole(shape) for shape in shapes],
        scratch_shapes=[pltpu.VMEM((HD, total), BF16), *scratch],
        compiler_params=params(),
        cost_estimate=cost(8 * total * size * HD, 2 * total * size),
    )(packed, weights, inverse, out, own, got, after, *before)


def per_device(queries, keys, values, out_grad, gate, proj_weight, lengths):
    seq, dp = lax.axis_size("seq"), lax.axis_size("dp")
    rows = queries.shape[0]
    wrows = proj_weight.shape[0]
    swap = [(0, 1), (1, 0)]
    right = [(i, (i + 1) % seq) for i in range(seq)]
    left = [(i, (i - 1) % seq) for i in range(seq)]

    def move(array, step):
        return lax.ppermute(array, "seq", right if step > 0 else left)

    own_rows = scale(out_grad, gate, lengths)
    from_left, from_right = move(own_rows, 1), move(own_rows, -1)
    near = [from_left, from_right]
    left_top, left_low, right_top, right_low = halves(from_left, from_right)
    for i in range(2):
        left_top, right_low = move(left_top, 1), move(right_low, -1)
        left_low, right_top = move(left_low, 1), move(right_top, -1)
        if (HOLD2, HOLD3)[i]:
            if i == 0:
                (left_top,) = hold((left_top,), HOLD2)
            else:
                (left_low,) = hold((left_low,), HOLD3)
        near += [left_top, left_low, right_top, right_low]

    packed = lax.all_to_all(
        pack(queries, keys, values, proj_weight, seq), "seq", split_axis=0, concat_axis=0, tiled=True
    )
    copies = spread(packed, rows, wrows, dp, packed)
    own_weight = lax.all_to_all(copies, "dp", split_axis=0, concat_axis=0, tiled=True).reshape(-1, HD)
    other_weight = lax.ppermute(own_weight, "tensor", swap)

    *state, low = attend_forward(packed, lengths, rows, copies)
    low_other = lax.ppermute(low, "tensor", swap)

    left_top, right_low, low = lax.optimization_barrier((left_top, right_low, low))
    far = [move(left_top, 1), move(right_low, -1)]
    last = [own_rows, *far]

    near_own, other = project(near, own_weight, other_weight, left_top)
    near_got = lax.ppermute(other, "tensor", swap)
    proj_own, proj_send = weight_grad(low, low_other, [*near, *last], near_own)
    proj_got = lax.ppermute(proj_send, "tensor", swap)
    own, other = project(last, own_weight, other_weight, proj_own)
    got = lax.ppermute(other, "tensor", swap)
    joined = join(proj_own, proj_got, own).reshape(dp, seq * wrows, HD)
    parts = lax.all_to_all(joined, "dp", split_axis=0, concat_axis=0, tiled=True)

    query_rows, *sums = attend_backward(packed, state, near_own, near_got, rows, 0, [], joined)
    grads = attend_backward(packed, state, own, got, rows, 6, [*sums, query_rows], joined)[0]
    result = finish(grads, parts, packed.shape[1] - 3 * rows)
    result = lax.all_to_all(result, "seq", split_axis=0, concat_axis=0, tiled=True)
    return tuple(unpack(result, rows, wrows))


def solution(mesh):
    token = P(("dp", "seq"), "tensor")
    return jax.shard_map(
        per_device,
        mesh=mesh,
        in_specs=(token, token, token, token, P("dp", None), token, P("dp")),
        out_specs=(token, token, token, token),
        check_vma=False,
    )
```
